32 devices in a mesh: groups: 2 (over x), gx: 16 (over z, y, core).
Axes of the slice: x: 2, y: 2, z: 4, core: 2. Of those that a mesh axis runs over, the one named last changes fastest.
Arguments:
- hidden_state: bfloat16 [320, 18432], P('groups', 'gx'), parts along dimension 0, may hold values from -80 to 80
- norm_gain: float32 [18432], P('gx'), may hold values from 0.1 to 1.9
- query_weight: bfloat16 [18432, 8192], P(None, 'gx'), may hold values from -0.046875 to 0.046875
- keyval_weight: bfloat16 [18432, 512], P('gx'), may hold values from -0.046875 to 0.046875
- out_weight: bfloat16 [8192, 18432], P('gx'), may hold values from -0.25 to 0.25
- cache_entries: bfloat16 [320, 512, 512], P(('groups', 'gx')), parts along dimension 0, may hold values from -400 to 400
- cache_lengths: int32 [320], P(('groups', 'gx')), parts along dimension 0, may hold values from 2 to 511, as said below
Outputs:
- layer_out: bfloat16 [320, 18432], P('groups', 'gx'), parts along dimension 0
The draws below stay inside these ranges and needn't reach their ends.
There are 2 independent parts, one for each index of `groups`. The reference program is written for one: setup_inputs(seed, part) draws one part's arguments, and reference() takes and returns one part's arrays. A program takes and returns all parts, laid end to end along the dimension named above; an argument that names none is the same for every part. Nothing has to cross between parts.
Inputs may be any that keep to these rules, and one draw needn't show every extreme that they name: `cache_lengths`: slots at or beyond a row's length hold entries that must be ignored.
All inputs are finite; a program needn't handle non-finite values.
Results may differ from the reference program's by a relative error of at most 0.012.
Values may be sent and summed in bfloat16 or wider, within the bound.
A program may use at most 128 MiB of HBM per device.

```python
import jax
import jax.numpy as jnp
from jax import lax

D = 18432
HQ = 32
HD = 256
LMAX = 512
B = 160


def draw_hidden_state(key, part):
    key = jax.random.fold_in(key, 1)
    first = jax.random.fold_in(key, 0)
    ramp = 1.0 + 2.0 * jnp.arange(D, dtype=jnp.float32) / (D - 1)
    result = jnp.clip(jax.random.normal(first, (B, D), jnp.float32), -6.0, 6.0) * ramp
    return result.astype(jnp.bfloat16)


def draw_cache_entries(key, part):
    key = jax.random.fold_in(key, 2)
    first = jax.random.fold_in(key, 0)
    result = jnp.clip(jax.random.normal(first, (B, LMAX, 2 * HD), jnp.float32), -6.0, 6.0)
    return result.astype(jnp.bfloat16)


def draw_cache_lengths(key, part):
    key = jax.random.fold_in(key, 3)
    first, second = jax.random.split(key)
    drawn = jax.random.randint(first, (B,), 2, LMAX)
    chosen = jax.random.randint(second, (), 0, B)
    return jnp.where(jnp.arange(B) == chosen, LMAX - 1, drawn).astype(jnp.int32)


def block_scale(key, extent, cuts, smallest, high):
    def one(position, shards_of):
        steps = jax.random.uniform(jax.random.fold_in(jax.random.fold_in(key, 6), position), (shards_of,), jnp.float32, smallest / len(cuts), high / len(cuts))
        return jnp.repeat(jnp.exp(steps), extent[position] // shards_of).reshape((-1,) + (1,) * (len(extent) - position - 1))

    gain = one(*cuts[0])
    for cut in cuts[1:]:
        gain = gain * one(*cut)
    return gain


def bell_draw(own_key, extent, scale, most, cuts=(), kind=jnp.bfloat16):
    factor_of = block_scale(own_key, extent, cuts, -0.22, 0.18) if cuts else 1.0
    values = jax.random.normal(own_key, extent, jnp.float32) * scale * factor_of
    return jnp.minimum(jnp.maximum(values, -most), most).astype(kind)


def setup_inputs(seed: int = 0, part: int = 0) -> dict:
    seeds = jax.random.split(jax.random.key(seed), 8)
    part_keys = jax.random.split(jax.random.fold_in(seeds[7], part), 8)
    return {
        "hidden_state": draw_hidden_state(jax.random.fold_in(jax.random.fold_in(seeds[7], part), 71), part),
        "norm_gain": jnp.clip(1.0 + 0.18 * jax.random.normal(seeds[1], (D,), jnp.float32), 0.1, 1.9),
        "query_weight": bell_draw(seeds[2], (D, HQ * HD), D ** -0.5, 0.046875, ((1, 16),)),
        "keyval_weight": bell_draw(seeds[3], (D, 2 * HD), D ** -0.5, 0.046875, ((0, 16),)),
        "out_weight": bell_draw(seeds[4], (HQ * HD, D), (HQ * HD // 16) ** -0.5, 0.25, ((0, 16),)),
        "cache_entries": draw_cache_entries(jax.random.fold_in(jax.random.fold_in(seeds[7], part), 71), part),
        "cache_lengths": draw_cache_lengths(jax.random.fold_in(jax.random.fold_in(seeds[7], part), 71), part),
    }


def reference(hidden_state, norm_gain, query_weight, keyval_weight, out_weight, cache_entries, cache_lengths):
    state32 = hidden_state.astype(jnp.float32)
    row_mean = lax.optimization_barrier(jnp.sum(state32, axis=1)) / D
    row_var = lax.optimization_barrier(jnp.sum(state32 * state32, axis=1)) / D - row_mean * row_mean
    normed = ((state32 - row_mean[:, None]) * lax.rsqrt(row_var + 1e-05)[:, None] * norm_gain).astype(jnp.bfloat16)
    query = (jnp.dot(normed, query_weight, preferred_element_type=jnp.float32) * HD ** (-0.5)).astype(jnp.bfloat16)
    new_entry = jnp.dot(normed, keyval_weight, preferred_element_type=jnp.float32).astype(jnp.bfloat16)
    query3 = query.reshape(B, HQ, HD).astype(jnp.float32)
    keys = cache_entries[:, :, :HD].astype(jnp.float32)
    values = cache_entries[:, :, HD:].astype(jnp.float32)
    scores = jnp.einsum('bhd,bld->bhl', query3, keys)
    fresh = jnp.einsum('bhd,bd->bh', query3, new_entry[:, :HD].astype(jnp.float32))
    valid = jnp.arange(LMAX)[None, :] < cache_lengths[:, None]
    scores = jnp.where(valid[:, None, :], scores, -1e+30)
    peak = jnp.maximum(lax.optimization_barrier(jnp.max(scores, axis=-1)), fresh)
    weights = jnp.exp(scores - peak[..., None]) * valid[:, None, :].astype(jnp.float32)
    fresh_w = jnp.exp(fresh - peak)
    total = lax.optimization_barrier(jnp.sum(weights, axis=-1)) + fresh_w
    probs = (weights / total[..., None]).astype(jnp.bfloat16)
    fresh_p = (fresh_w / total).astype(jnp.bfloat16)
    mixed = jnp.einsum('bhl,bld->bhd', probs.astype(jnp.float32), values)
    mixed = mixed + fresh_p.astype(jnp.float32)[..., None] * new_entry[:, None, HD:].astype(jnp.float32)
    attended = mixed.reshape(B, HQ * HD).astype(jnp.bfloat16)
    delta = jnp.dot(attended, out_weight, preferred_element_type=jnp.float32)
    return (state32 + delta).astype(jnp.bfloat16)
```

```python
import jax
import jax.numpy as jnp
from jax import lax
from jax.experimental import pallas as pl
from jax.experimental.pallas import tpu as pltpu
from jax.sharding import PartitionSpec as P


def plain_device(
    hidden_state, norm_gain, query_weight, keyval_weight, out_weight, cache_entries, cache_lengths
):
    members = lax.axis_size("gx")
    rows_all = hidden_state.shape[0]
    width_local = hidden_state.shape[1]
    width = width_local * members
    rows_local = rows_all // members
    head_size = keyval_weight.shape[1] // 2
    state32 = hidden_state.astype(jnp.float32)
    row_total, row_squares = lax.psum(
        (jnp.sum(state32, axis=1), jnp.sum(state32 * state32, axis=1)), "gx"
    )
    row_mean = row_total / width
    row_var = row_squares / width - row_mean * row_mean
    normed_local = (
        (state32 - row_mean[:, None]) * lax.rsqrt(row_var + 1e-05)[:, None] * norm_gain
    ).astype(jnp.bfloat16)
    query_sum = jnp.dot(
        lax.all_gather(normed_local, "gx", axis=1, tiled=True),
        query_weight,
        preferred_element_type=jnp.float32,
    )
    query = (query_sum * head_size ** (-0.5)).astype(jnp.bfloat16)
    new_entry = lax.psum_scatter(
        jnp.dot(normed_local, keyval_weight, preferred_element_type=jnp.float32).astype(
            jnp.bfloat16
        ),
        "gx",
        scatter_dimension=0,
        tiled=True,
    )
    query_rows = lax.all_to_all(query, "gx", split_axis=0, concat_axis=1, tiled=True)
    heads_all = query_rows.shape[1] // head_size
    query3 = query_rows.reshape(rows_local, heads_all, head_size)
    keys = cache_entries[:, :, :head_size]
    values = cache_entries[:, :, head_size:]
    scores = jnp.einsum("rhd,rld->rhl", query3, keys, preferred_element_type=jnp.float32)
    fresh = jnp.einsum(
        "rhd,rd->rh", query3, new_entry[:, :head_size], preferred_element_type=jnp.float32
    )
    valid = jnp.arange(keys.shape[1])[None, :] < cache_lengths[:, None]
    scores = jnp.where(valid[:, None, :], scores, -1e30)
    peak = jnp.maximum(jnp.max(scores, axis=-1), fresh)
    weights = jnp.exp(scores - peak[..., None]) * valid[:, None, :].astype(jnp.float32)
    fresh_w = jnp.exp(fresh - peak)
    total = jnp.sum(weights, axis=-1) + fresh_w
    probs = (weights / total[..., None]).astype(jnp.bfloat16)
    fresh_p = (fresh_w / total).astype(jnp.bfloat16)
    mixed = jnp.einsum("rhl,rld->rhd", probs, values, preferred_element_type=jnp.float32)
    mixed = mixed + fresh_p.astype(jnp.float32)[..., None] * new_entry[:, None, head_size:].astype(
        jnp.float32
    )
    attended_rows = mixed.reshape(rows_local, heads_all * head_size).astype(jnp.bfloat16)
    attended = lax.all_to_all(attended_rows, "gx", split_axis=1, concat_axis=0, tiled=True)
    partial_out = jnp.dot(attended, out_weight, preferred_element_type=jnp.float32)
    summed = lax.psum_scatter(
        partial_out.astype(jnp.bfloat16), "gx", scatter_dimension=1, tiled=True
    ).astype(jnp.float32)
    return (hidden_state.astype(jnp.float32) + summed).astype(jnp.bfloat16)


MESH = pl.DeviceIdType.MESH
PAD = 16
DEPTH = 4


def remote(src, dst, send, recv, peer):
    return pltpu.make_async_remote_copy(
        src_ref=src,
        dst_ref=dst,
        send_sem=send,
        recv_sem=recv,
        device_id={"gx": peer},
        device_id_type=MESH,
    )


def meet_all(members, me):
    barrier = pltpu.get_barrier_semaphore()
    for k in range(1, members):
        pl.semaphore_signal(
            barrier, inc=1, device_id={"gx": (me + k) % members}, device_id_type=MESH
        )
    pl.semaphore_wait(barrier, members - 1)


def place():
    me = lax.axis_index("gx")
    return me, me // 4, (me // 2) % 2, me % 2


def far_to_near(z):
    first = 3 * (1 - z // 2)
    third = 1 + z % 2
    return [first, 6 - z - first - third, third, z]


def slot_of(z, y, c):
    return z * 4 + y * 2 + c


def query_kernel(
    head_scale,
    x_ref,
    note_ref,
    wq_hbm,
    kvw_ref,
    sel_ref,
    q_out,
    kv_out,
    buf,
    notes,
    wbuf,
    acc,
    stat,
    q_send,
    q_got,
    kv_send,
    kv_got,
    w_sem,
    own_sem,
    z_sem,
    y_sem,
    c_sem,
    recv_sem,
    note_sem,
    kv_sem,
    q_sem,
):
    members = buf.shape[0]
    rows, width = x_ref.shape
    total_width = width * members
    me, z, y, c = place()
    sibling = slot_of(z, y, 1 - c)
    across = slot_of(z, 1 - y, c)
    above = slot_of(jnp.minimum(z + 1, DEPTH - 1), y, c)
    below = slot_of(jnp.maximum(z - 1, 0), y, c)

    def weights_copy(slot):
        start = pl.multiple_of(slot * width, 128)
        return pltpu.make_async_copy(
            wq_hbm.at[pl.ds(start, width), :], wbuf.at[slot], w_sem.at[slot]
        )

    own = pltpu.make_async_copy(x_ref, buf.at[me], own_sem)
    own.start()
    notes[me] = note_ref[...]
    order = far_to_near(z)[::-1]
    own.wait()
    meet_all(members, me)

    def shard(slot, send, peer):
        return remote(buf.at[slot], buf.at[slot], send, recv_sem.at[slot], peer)

    def up(zz):
        return shard(slot_of(zz, y, c), z_sem.at[0, zz], above)

    def down(zz):
        return shard(slot_of(zz, y, c), z_sem.at[1, zz], below)

    def over(zz):
        return shard(slot_of(zz, y, c), y_sem.at[zz], across)

    def aside(zz, yy):
        return shard(slot_of(zz, yy, c), c_sem.at[zz * 2 + yy], sibling)

    def arrived(slot):
        shard(slot, own_sem, sibling).wait_recv()

    def spread(src_of, dst, sems):
        for k in range(1, members):
            peer = (me + k) % members
            remote(src_of(peer), dst.at[me], sems.at[0, peer], sems.at[1, me], peer).start()

    def collect(src_of, dst, sems):
        for k in range(1, members):
            peer = (me + k) % members
            remote(src_of(peer), dst.at[peer], sems.at[0, peer], sems.at[1, peer], peer).wait()

    spread(lambda peer: note_ref, notes, note_sem)
    over(z).start()

    @pl.when(z < DEPTH - 1)
    def _():
        up(z).start()

    @pl.when(z > 0)
    def _():
        down(z).start()

    aside(z, y).start()
    for slot in range(members):
        weights_copy(slot).start()
    collect(lambda peer: note_ref, notes, note_sem)

    mean = jnp.sum(notes[:, 0:2, :], axis=0) / total_width
    var = jnp.sum(notes[:, 2:4, :], axis=0) / total_width - mean * mean
    inv = lax.rsqrt(var + 1e-05)
    stat[0, 0:128, :] = jnp.broadcast_to(mean[0:1, :], (128, 128)).T
    stat[1, 0:128, :] = jnp.broadcast_to(inv[0:1, :], (128, 128)).T
    stat[0, 128:rows, :] = jnp.broadcast_to(mean[1:2, :], (128, 128)).T[0 : rows - 128]
    stat[1, 128:rows, :] = jnp.broadcast_to(inv[1:2, :], (128, 128)).T[0 : rows - 128]

    def normed(slot):
        tiles = []
        for t in range(width // 128):
            part = buf[slot, :, t * 128 : (t + 1) * 128].astype(jnp.float32)
            gain = notes[slot, 4 + t : 5 + t, :]
            tiles.append(((part - stat[0]) * stat[1] * gain).astype(jnp.bfloat16))
        return jnp.concatenate(tiles, axis=1)

    kv = jnp.dot(normed(me), kvw_ref[...], preferred_element_type=jnp.float32)
    kv = jnp.dot(sel_ref[...], kv.astype(jnp.bfloat16), preferred_element_type=jnp.float32)
    kv_send[...] = kv.astype(jnp.bfloat16).reshape(kv_send.shape)
    spread(lambda peer: kv_send.at[peer], kv_got, kv_sem)
    kv_got[me] = kv_send[me]
    acc[...] = jnp.zeros_like(acc)

    def work(zz, yy):
        def one(k, carry):
            slot = slot_of(zz, yy, (c + k) % 2)

            @pl.when(k == 1)
            def _():
                arrived(slot)

            weights_copy(slot).wait()
            acc[...] += jnp.dot(normed(slot), wbuf[slot], preferred_element_type=jnp.float32)
            return carry

        lax.fori_loop(0, 2, one, 0)

    work(z, y)
    for i in range(1, DEPTH):

        @pl.when(z - i >= 0)
        def _():
            arrived(slot_of(jnp.maximum(z - i, 0), y, c))

            @pl.when(z < DEPTH - 1)
            def _():
                up(jnp.maximum(z - i, 0)).start()

        @pl.when(z + i < DEPTH)
        def _():
            arrived(slot_of(jnp.minimum(z + i, DEPTH - 1), y, c))

            @pl.when(z > 0)
            def _():
                down(jnp.minimum(z + i, DEPTH - 1)).start()

        over(order[i]).start()
        aside(order[i], y).start()
        arrived(slot_of(order[i - 1], 1 - y, c))
        aside(order[i - 1], 1 - y).start()
        work(order[i], y)
        work(order[i - 1], 1 - y)
    arrived(slot_of(order[DEPTH - 1], 1 - y, c))
    aside(order[DEPTH - 1], 1 - y).start()
    work(order[DEPTH - 1], 1 - y)

    query = (acc[...] * head_scale).astype(jnp.bfloat16)
    query = jnp.dot(sel_ref[...], query, preferred_element_type=jnp.float32)
    q_send[...] = query.astype(jnp.bfloat16).reshape(q_send.shape)
    spread(lambda peer: q_send.at[peer], q_got, q_sem)
    q_got[me] = q_send[me]
    collect(lambda peer: kv_send.at[peer], kv_got, kv_sem)
    kv_out[...] = jnp.sum(kv_got[...].astype(jnp.float32), axis=0).astype(jnp.bfloat16)
    for zz in range(DEPTH):
        over(zz).wait_send()
        aside(zz, 0).wait_send()
        aside(zz, 1).wait_send()

        @pl.when((z < DEPTH - 1) & (zz <= z))
        def _():
            up(zz).wait_send()

        @pl.when((z > 0) & (zz >= z))
        def _():
            down(zz).wait_send()

    collect(lambda peer: q_send.at[peer], q_got, q_sem)
    q_out[...] = q_got[...]


def query_call(x, note, wq, kvw, sel, members, head_scale):
    rows, width = x.shape
    cols = wq.shape[1]
    vmem = pl.BlockSpec(memory_space=pltpu.VMEM)
    swap = (members, PAD, cols)
    kv_cols = kvw.shape[1]
    dma = pltpu.SemaphoreType.DMA
    return pl.pallas_call(
        lambda *refs: query_kernel(head_scale, *refs),
        out_shape=(
            jax.ShapeDtypeStruct(swap, jnp.bfloat16),
            jax.ShapeDtypeStruct((PAD, kv_cols), jnp.bfloat16),
        ),
        in_specs=[vmem, vmem, pl.BlockSpec(memory_space=pl.ANY), vmem, vmem],
        out_specs=(vmem, vmem),
        scratch_shapes=[
            pltpu.VMEM((members, rows, width), jnp.bfloat16),
            pltpu.VMEM((members,) + note.shape, jnp.float32),
            pltpu.VMEM((members, width, cols), jnp.bfloat16),
            pltpu.VMEM((rows, cols), jnp.float32),
            pltpu.VMEM((2, rows, 128), jnp.float32),
            pltpu.VMEM(swap, jnp.bfloat16),
            pltpu.VMEM(swap, jnp.bfloat16),
            pltpu.VMEM((members, PAD, kv_cols), jnp.bfloat16),
            pltpu.VMEM((members, PAD, kv_cols), jnp.bfloat16),
            dma((members,)),
            dma,
            dma((2, DEPTH)),
            dma((DEPTH,)),
            dma((2 * DEPTH,)),
            dma((members,)),
            dma((2, members)),
            dma((2, members)),
            dma((2, members)),
        ],
        compiler_params=pltpu.CompilerParams(
            collective_id=0, has_side_effects=True, vmem_limit_bytes=48 * 1024 * 1024
        ),
    )(x, note, wq, kvw, sel)


def output_kernel(
    att_ref,
    pick_ref,
    wo_hbm,
    out_ref,
    att_got,
    att,
    wbuf,
    mine,
    c_send,
    c_got,
    y_send,
    y_got,
    z_send,
    z_got,
    w_sem,
    att_sem,
    c_sem,
    y_sem,
    z_sem,
):
    members = att_ref.shape[0]
    rows, width = out_ref.shape
    me, z, y, c = place()
    sibling = slot_of(z, y, 1 - c)
    across = slot_of(z, 1 - y, c)
    above = slot_of(jnp.minimum(z + 1, DEPTH - 1), y, c)
    below = slot_of(jnp.maximum(z - 1, 0), y, c)
    order = far_to_near(z)

    def weights_copy(slot):
        start = pl.multiple_of(slot * width, 128)
        return pltpu.make_async_copy(
            wo_hbm.at[:, pl.ds(start, width)], wbuf.at[slot], w_sem.at[slot]
        )

    for zz in order:
        for yy in (1 - y, y):
            for cc in (1 - c, c):
                weights_copy(slot_of(zz, yy, cc)).start()
    meet_all(members, me)

    def swap(k):
        peer = (me + k) % members
        return peer, att_ref.at[peer], att_sem.at[0, peer]

    for k in range(1, members):
        peer, src, sem = swap(k)
        remote(src, att_got.at[me], sem, att_sem.at[1, me], peer).start()
    att_got[me] = att_ref[me]
    for k in range(1, members):
        peer, src, sem = swap(k)
        remote(src, att_got.at[peer], sem, att_sem.at[1, peer], peer).wait()
    gathered = att_got[...].reshape(members * PAD, att.shape[1])
    att[...] = jnp.dot(
        pick_ref[...], gathered, preferred_element_type=jnp.float32
    ).astype(jnp.bfloat16)

    tile = width // 3 if width % 384 == 0 else width

    def product(slot, store):
        weights_copy(slot).wait()

        def one(t, carry):
            cols = pl.ds(pl.multiple_of(t * tile, 128), tile)
            store(
                cols, jnp.dot(att[...], wbuf[slot, :, cols], preferred_element_type=jnp.float32)
            )
            return carry

        lax.fori_loop(0, width // tile, one, 0)

    def aside(p):
        return remote(c_send.at[p], c_got.at[p], c_sem.at[0, p], c_sem.at[1, p], sibling)

    def over(i):
        return remote(y_send.at[i], y_got.at[i], y_sem.at[0, i], y_sem.at[1, i], across)

    def up(zz):
        return remote(
            z_send.at[zz], z_got.at[0, zz], z_sem.at[0, zz], z_sem.at[1, zz], above
        )

    def down(zz):
        return remote(
            z_send.at[zz], z_got.at[1, zz], z_sem.at[0, zz], z_sem.at[2, zz], below
        )

    for i in range(DEPTH):
        for j, yy in enumerate((1 - y, y)):
            p = 2 * i + j

            def to_sibling(cols, value):
                c_send[p, :, cols] = value.astype(jnp.bfloat16)

            product(slot_of(order[i], yy, 1 - c), to_sibling)
            aside(p).start()
        for j, yy in enumerate((1 - y, y)):
            p = 2 * i + j

            def keep(cols, value):
                mine[i, :, cols] = value

            product(slot_of(order[i], yy, c), keep)
            aside(p).wait_recv()
            if j == 0:
                y_send[i] = (mine[i] + c_got[p].astype(jnp.float32)).astype(jnp.bfloat16)
                over(i).start()
            else:
                mine[i] += c_got[p].astype(jnp.float32)

    for i in range(DEPTH - 1):
        zz = order[i]
        over(i).wait_recv()
        mine[i] += y_got[i].astype(jnp.float32)

        @pl.when(zz > z)
        def _():
            @pl.when(z > 0)
            def _():
                up(zz).wait_recv()
                mine[i] += z_got[0, zz].astype(jnp.float32)

            z_send[zz] = mine[i].astype(jnp.bfloat16)
            up(zz).start()

        @pl.when(zz < z)
        def _():
            @pl.when(z < DEPTH - 1)
            def _():
                down(zz).wait_recv()
                mine[i] += z_got[1, zz].astype(jnp.float32)

            z_send[zz] = mine[i].astype(jnp.bfloat16)
            down(zz).start()

    last = DEPTH - 1
    over(last).wait_recv()
    mine[last] += y_got[last].astype(jnp.float32)

    @pl.when(z > 0)
    def _():
        up(z).wait_recv()
        mine[last] += z_got[0, z].astype(jnp.float32)

    @pl.when(z < DEPTH - 1)
    def _():
        down(z).wait_recv()
        mine[last] += z_got[1, z].astype(jnp.float32)

    out_ref[...] = mine[last]
    for i in range(DEPTH):
        over(i).wait_send()
        aside(2 * i).wait_send()
        aside(2 * i + 1).wait_send()
    for i in range(DEPTH - 1):
        up(order[i]).wait_send()


def output_call(att, pick, wo, members, width):
    rows = pick.shape[0]
    depth = wo.shape[0]
    vmem = pl.BlockSpec(memory_space=pltpu.VMEM)
    dma = pltpu.SemaphoreType.DMA
    block = (rows, width)
    return pl.pallas_call(
        output_kernel,
        out_shape=jax.ShapeDtypeStruct(block, jnp.float32),
        in_specs=[vmem, vmem, pl.BlockSpec(memory_space=pl.ANY)],
        out_specs=vmem,
        scratch_shapes=[
            pltpu.VMEM(att.shape, jnp.bfloat16),
            pltpu.VMEM((rows, depth), jnp.bfloat16),
            pltpu.VMEM((members, depth, width), jnp.bfloat16),
            pltpu.VMEM((DEPTH,) + block, jnp.float32),
            pltpu.VMEM((2 * DEPTH,) + block, jnp.bfloat16),
            pltpu.VMEM((2 * DEPTH,) + block, jnp.bfloat16),
            pltpu.VMEM((DEPTH,) + block, jnp.bfloat16),
            pltpu.VMEM((DEPTH,) + block, jnp.bfloat16),
            pltpu.VMEM((DEPTH,) + block, jnp.bfloat16),
            pltpu.VMEM((2, DEPTH) + block, jnp.bfloat16),
            dma((members,)),
            dma((2, members)),
            dma((2, 2 * DEPTH)),
            dma((2, DEPTH)),
            dma((3, DEPTH)),
        ],
        compiler_params=pltpu.CompilerParams(
            collective_id=1, has_side_effects=True, vmem_limit_bytes=56 * 1024 * 1024
        ),
    )(att, pick, wo)


def attention(query3, new_entry, cache_entries, cache_lengths):
    head_size = query3.shape[2]
    keys = cache_entries[:, :, :head_size]
    values = cache_entries[:, :, head_size:]
    scores = jnp.einsum("rhd,rld->rhl", query3, keys, preferred_element_type=jnp.float32)
    fresh = jnp.einsum(
        "rhd,rd->rh", query3, new_entry[:, :head_size], preferred_element_type=jnp.float32
    )
    valid = jnp.arange(keys.shape[1])[None, :] < cache_lengths[:, None]
    scores = jnp.where(valid[:, None, :], scores, -1e30)
    peak = jnp.maximum(jnp.max(scores, axis=-1), fresh)
    weights = jnp.exp(scores - peak[..., None]) * valid[:, None, :].astype(jnp.float32)
    fresh_w = jnp.exp(fresh - peak)
    total = jnp.sum(weights, axis=-1) + fresh_w
    probs = (weights / total[..., None]).astype(jnp.bfloat16)
    fresh_p = (fresh_w / total).astype(jnp.bfloat16)
    mixed = jnp.einsum("rhl,rld->rhd", probs, values, preferred_element_type=jnp.float32)
    mixed = mixed + fresh_p.astype(jnp.float32)[..., None] * new_entry[:, None, head_size:].astype(
        jnp.float32
    )
    return mixed.astype(jnp.bfloat16)


def fast_device(
    hidden_state, norm_gain, query_weight, keyval_weight, out_weight, cache_entries, cache_lengths
):
    members = lax.axis_size("gx")
    rows_all, width = hidden_state.shape
    rows = rows_all // members
    head_size = keyval_weight.shape[1] // 2
    cols = query_weight.shape[1]
    state32 = hidden_state.astype(jnp.float32)
    sums = jnp.stack([jnp.sum(state32, axis=1), jnp.sum(state32 * state32, axis=1)])
    sums = jnp.pad(sums, ((0, 0), (0, 256 - rows_all))).reshape(4, 128)
    note = jnp.concatenate([sums, norm_gain.reshape(-1, 128)], axis=0)
    note = jnp.pad(note, ((0, -note.shape[0] % 8), (0, 0)))
    padded = jnp.arange(members * PAD)
    source = jnp.where(padded % PAD < rows, padded // PAD * rows + padded % PAD, -1)
    select = (source[:, None] == jnp.arange(rows_all)[None, :]).astype(jnp.bfloat16)
    pick = (source[None, :] == jnp.arange(rows_all)[:, None]).astype(jnp.bfloat16)
    q_rows, kv_rows = query_call(
        hidden_state, note, query_weight, keyval_weight, select, members, head_size ** (-0.5)
    )
    query3 = q_rows[:, :rows].transpose(1, 0, 2).reshape(rows, -1, head_size)
    mixed = attention(query3, kv_rows[:rows], cache_entries, cache_lengths)
    att = mixed.reshape(rows, members, cols).transpose(1, 0, 2)
    att = jnp.pad(att, ((0, 0), (0, PAD - rows), (0, 0)))
    summed = output_call(att, pick, out_weight, members, width)
    return (hidden_state.astype(jnp.float32) + summed).astype(jnp.bfloat16)


def on_device(hidden_state, *others):
    members = lax.axis_size("gx")
    rows_all, width = hidden_state.shape
    fits = width % 128 == 0 and 128 < rows_all <= 256 and rows_all % 16 == 0
    if members == 4 * DEPTH and fits and rows_all // members <= PAD:
        return fast_device(hidden_state, *others)
    return plain_device(hidden_state, *others)


def solution(mesh):
    in_specs = (
        P("groups", "gx"),
        P("gx"),
        P(None, "gx"),
        P("gx", None),
        P("gx", None),
        P(("groups", "gx"), None, None),
        P(("groups", "gx")),
    )
    out_specs = P("groups", "gx")
    return jax.shard_map(
        on_device, mesh=mesh, in_specs=in_specs, out_specs=out_specs, check_vma=False
    )
```

```python
import jax
import jax.numpy as jnp
from jax import lax
from jax.experimental import pallas as pl
from jax.experimental.pallas import tpu as pltpu
from jax.sharding import PartitionSpec as P


def plain_device(
    hidden_state, norm_gain, query_weight, keyval_weight, out_weight, cache_entries, cache_lengths
):
    members = lax.axis_size("gx")
    rows_all = hidden_state.shape[0]
    width_local = hidden_state.shape[1]
    width = width_local * members
    rows_local = rows_all // members
    head_size = keyval_weight.shape[1] // 2
    state32 = hidden_state.astype(jnp.float32)
    row_total, row_squares = lax.psum(
        (jnp.sum(state32, axis=1), jnp.sum(state32 * state32, axis=1)), "gx"
    )
    row_mean = row_total / width
    row_var = row_squares / width - row_mean * row_mean
    normed_local = (
        (state32 - row_mean[:, None]) * lax.rsqrt(row_var + 1e-05)[:, None] * norm_gain
    ).astype(jnp.bfloat16)
    query_sum = jnp.dot(
        lax.all_gather(normed_local, "gx", axis=1, tiled=True),
        query_weight,
        preferred_element_type=jnp.float32,
    )
    query = (query_sum * head_size ** (-0.5)).astype(jnp.bfloat16)
    new_entry = lax.psum_scatter(
        jnp.dot(normed_local, keyval_weight, preferred_element_type=jnp.float32).astype(
            jnp.bfloat16
        ),
        "gx",
        scatter_dimension=0,
        tiled=True,
    )
    query_rows = lax.all_to_all(query, "gx", split_axis=0, concat_axis=1, tiled=True)
    heads_all = query_rows.shape[1] // head_size
    query3 = query_rows.reshape(rows_local, heads_all, head_size)
    keys = cache_entries[:, :, :head_size]
    values = cache_entries[:, :, head_size:]
    scores = jnp.einsum("rhd,rld->rhl", query3, keys, preferred_element_type=jnp.float32)
    fresh = jnp.einsum(
        "rhd,rd->rh", query3, new_entry[:, :head_size], preferred_element_type=jnp.float32
    )
    valid = jnp.arange(keys.shape[1])[None, :] < cache_lengths[:, None]
    scores = jnp.where(valid[:, None, :], scores, -1e30)
    peak = jnp.maximum(jnp.max(scores, axis=-1), fresh)
    weights = jnp.exp(scores - peak[..., None]) * valid[:, None, :].astype(jnp.float32)
    fresh_w = jnp.exp(fresh - peak)
    total = jnp.sum(weights, axis=-1) + fresh_w
    probs = (weights / total[..., None]).astype(jnp.bfloat16)
    fresh_p = (fresh_w / total).astype(jnp.bfloat16)
    mixed = jnp.einsum("rhl,rld->rhd", probs, values, preferred_element_type=jnp.float32)
    mixed = mixed + fresh_p.astype(jnp.float32)[..., None] * new_entry[:, None, head_size:].astype(
        jnp.float32
    )
    attended_rows = mixed.reshape(rows_local, heads_all * head_size).astype(jnp.bfloat16)
    attended = lax.all_to_all(attended_rows, "gx", split_axis=1, concat_axis=0, tiled=True)
    partial_out = jnp.dot(attended, out_weight, preferred_element_type=jnp.float32)
    summed = lax.psum_scatter(
        partial_out.astype(jnp.bfloat16), "gx", scatter_dimension=1, tiled=True
    ).astype(jnp.float32)
    return (hidden_state.astype(jnp.float32) + summed).astype(jnp.bfloat16)


MESH = pl.DeviceIdType.MESH
PAD = 16
DEPTH = 4
FIRST = 32


def remote(src, dst, send, recv, peer):
    return pltpu.make_async_remote_copy(
        src_ref=src,
        dst_ref=dst,
        send_sem=send,
        recv_sem=recv,
        device_id={"gx": peer},
        device_id_type=MESH,
    )


def meet_all(members, me):
    barrier = pltpu.get_barrier_semaphore()
    for k in range(1, members):
        pl.semaphore_signal(
            barrier, inc=1, device_id={"gx": (me + k) % members}, device_id_type=MESH
        )
    pl.semaphore_wait(barrier, members - 1)


def place():
    me = lax.axis_index("gx")
    return me, me // 4, (me // 2) % 2, me % 2


def far_to_near(z):
    first = 3 * (1 - z // 2)
    third = 1 + z % 2
    return [first, 6 - z - first - third, third, z]


def pieces(rows):
    half = (rows - FIRST) // 2
    return [pl.ds(0, FIRST), pl.ds(FIRST, half), pl.ds(FIRST + half, half)]


def spread_rows(members, rows, local, flip):
    shape = (rows, members * PAD) if flip else (members * PAD, rows)
    p = lax.broadcasted_iota(jnp.int32, shape, 1 if flip else 0)
    r = lax.broadcasted_iota(jnp.int32, shape, 0 if flip else 1)
    inner = p & (PAD - 1)
    hit = (inner < local) & ((p >> 4) * local + inner == r)
    return jnp.where(hit, 1.0, 0.0).astype(jnp.bfloat16)


def slot_of(z, y, c):
    return z * 4 + y * 2 + c


def query_kernel(
    head_scale,
    x_hbm,
    note_ref,
    wq_hbm,
    kvw_hbm,
    q_out,
    kv_out,
    buf,
    notes,
    wbuf,
    kvw,
    acc,
    stat,
    q_send,
    q_got,
    kv_send,
    kv_got,
    w_sem,
    own_sem,
    z_sem,
    y_sem,
    c_sem,
    recv_sem,
    note_sem,
    kv_sem,
    q_sem,
):
    members = buf.shape[0]
    rows, width = x_hbm.shape
    parts = pieces(rows)
    total_width = width * members
    me, z, y, c = place()
    sibling = slot_of(z, y, 1 - c)
    across = slot_of(z, 1 - y, c)
    above = slot_of(jnp.minimum(z + 1, DEPTH - 1), y, c)
    below = slot_of(jnp.maximum(z - 1, 0), y, c)

    def weights_copy(slot):
        start = pl.multiple_of(slot * width, 128)
        return pltpu.make_async_copy(
            wq_hbm.at[pl.ds(start, width), :], wbuf.at[slot], w_sem.at[slot]
        )

    own = pltpu.make_async_copy(x_hbm, buf.at[me], own_sem.at[0])
    own.start()
    kvw_copy = pltpu.make_async_copy(kvw_hbm, kvw, own_sem.at[1])
    kvw_copy.start()
    notes[me] = note_ref[...]
    order = far_to_near(z)[::-1]
    own.wait()
    meet_all(members, me)

    def shard(slot, piece, send, peer):
        rows_of = pl.ds(0, rows) if piece == 3 else parts[piece]
        block = buf.at[slot, rows_of, :]
        return remote(block, block, send, recv_sem.at[slot, piece], peer)

    def up(zz, k):
        yy = 1 - y if k == 3 else y
        return shard(slot_of(zz, yy, c), k % 3, z_sem.at[0, zz, k], above)

    def down(zz, k):
        yy = 1 - y if k == 3 else y
        return shard(slot_of(zz, yy, c), k % 3, z_sem.at[1, zz, k], below)

    def over(zz, k):
        return shard(slot_of(zz, y, c), k, y_sem.at[zz, k], across)

    def aside(zz, yy):
        return shard(slot_of(zz, yy, c), 3, c_sem.at[zz * 2 + yy], sibling)

    def arrived(slot, piece):
        shard(slot, piece, own_sem.at[0], sibling).wait_recv()

    def both_ways(k):
        @pl.when(z < DEPTH - 1)
        def _():
            up(z, k).start()

        @pl.when(z > 0)
        def _():
            down(z, k).start()

    def relay(i, k):
        yy = 1 - y if k == 3 else y

        @pl.when(z - i >= 0)
        def _():
            low = jnp.maximum(z - i, 0)
            arrived(slot_of(low, yy, c), k % 3)

            @pl.when(z < DEPTH - 1)
            def _():
                up(low, k).start()

        @pl.when(z + i < DEPTH)
        def _():
            high = jnp.minimum(z + i, DEPTH - 1)
            arrived(slot_of(high, yy, c), k % 3)

            @pl.when(z > 0)
            def _():
                down(high, k).start()

    def spread(src_of, dst, sems):
        for k in range(1, members):
            peer = (me + k) % members
            remote(src_of(peer), dst.at[me], sems.at[0, peer], sems.at[1, me], peer).start()

    def collect(src_of, dst, sems):
        for k in range(1, members):
            peer = (me + k) % members
            remote(src_of(peer), dst.at[peer], sems.at[0, peer], sems.at[1, peer], peer).wait()

    spread(lambda peer: note_ref, notes, note_sem)
    over(z, 0).start()
    both_ways(1)
    over(z, 1).start()
    both_ways(2)
    over(z, 2).start()
    both_ways(0)
    aside(z, y).start()
    for slot in range(members):
        weights_copy(slot).start()
    collect(lambda peer: note_ref, notes, note_sem)

    mean = jnp.sum(notes[:, 0:2, :], axis=0) / total_width
    var = jnp.sum(notes[:, 2:4, :], axis=0) / total_width - mean * mean
    inv = lax.rsqrt(var + 1e-05)
    stat[0, 0:128, :] = jnp.broadcast_to(mean[0:1, :], (128, 128)).T
    stat[1, 0:128, :] = jnp.broadcast_to(inv[0:1, :], (128, 128)).T
    stat[0, 128:rows, :] = jnp.broadcast_to(mean[1:2, :], (128, 128)).T[0 : rows - 128]
    stat[1, 128:rows, :] = jnp.broadcast_to(inv[1:2, :], (128, 128)).T[0 : rows - 128]

    def normed(slot):
        tiles = []
        for t in range(width // 128):
            part = buf[slot, :, t * 128 : (t + 1) * 128].astype(jnp.float32)
            gain = notes[slot, 4 + t : 5 + t, :]
            tiles.append(((part - stat[0]) * stat[1] * gain).astype(jnp.bfloat16))
        return jnp.concatenate(tiles, axis=1)

    arrived(slot_of(z, 1 - y, c), 0)
    both_ways(3)
    kvw_copy.wait()
    select = spread_rows(members, rows, rows // members, False)
    kv = jnp.dot(normed(me), kvw[...], preferred_element_type=jnp.float32)
    kv = jnp.dot(select, kv.astype(jnp.bfloat16), preferred_element_type=jnp.float32)
    kv_send[...] = kv.astype(jnp.bfloat16).reshape(kv_send.shape)
    spread(lambda peer: kv_send.at[peer], kv_got, kv_sem)
    kv_got[me] = kv_send[me]
    acc[...] = jnp.zeros_like(acc)

    def work(zz, yy):
        def one(k, carry):
            slot = slot_of(zz, yy, (c + k) % 2)

            @pl.when(k == 1)
            def _():
                arrived(slot, 3)

            weights_copy(slot).wait()
            acc[...] += jnp.dot(normed(slot), wbuf[slot], preferred_element_type=jnp.float32)
            return carry

        lax.fori_loop(0, 2, one, 0)

    def finish_across(i):
        slot = slot_of(order[i], 1 - y, c)
        arrived(slot, 1)
        arrived(slot, 2)
        aside(order[i], 1 - y).start()

    for i in range(1, DEPTH):
        relay(i, 1)
        over(order[i], 1).start()
        work(order[i - 1], y)
        relay(i, 2)
        over(order[i], 2).start()
        finish_across(i - 1)
        relay(i, 0)
        aside(order[i], y).start()
        relay(i, 3)
        work(order[i - 1], 1 - y)
    work(order[DEPTH - 1], y)
    finish_across(DEPTH - 1)
    work(order[DEPTH - 1], 1 - y)

    query = (acc[...] * head_scale).astype(jnp.bfloat16)
    query = jnp.dot(select, query, preferred_element_type=jnp.float32)
    q_send[...] = query.astype(jnp.bfloat16).reshape(q_send.shape)
    spread(lambda peer: q_send.at[peer], q_got, q_sem)
    q_got[me] = q_send[me]
    collect(lambda peer: kv_send.at[peer], kv_got, kv_sem)
    kv_out[...] = jnp.sum(kv_got[...].astype(jnp.float32), axis=0).astype(jnp.bfloat16)
    for zz in range(DEPTH):
        for piece in range(3):
            over_sent = (piece > 0) | (zz == z)

            @pl.when(over_sent)
            def _():
                over(zz, piece).wait_send()

        aside(zz, 0).wait_send()
        aside(zz, 1).wait_send()

        @pl.when((z < DEPTH - 1) & (zz <= z))
        def _():
            for piece in range(4):
                up(zz, piece).wait_send()

        @pl.when((z > 0) & (zz >= z))
        def _():
            for piece in range(4):
                down(zz, piece).wait_send()

    collect(lambda peer: q_send.at[peer], q_got, q_sem)
    q_out[...] = q_got[...]


def query_call(x, note, wq, kvw, members, head_scale):
    rows, width = x.shape
    cols = wq.shape[1]
    vmem = pl.BlockSpec(memory_space=pltpu.VMEM)
    hbm = pl.BlockSpec(memory_space=pl.ANY)
    swap = (members, PAD, cols)
    kv_cols = kvw.shape[1]
    dma = pltpu.SemaphoreType.DMA
    return pl.pallas_call(
        lambda *refs: query_kernel(head_scale, *refs),
        out_shape=(
            jax.ShapeDtypeStruct(swap, jnp.bfloat16),
            jax.ShapeDtypeStruct((PAD, kv_cols), jnp.bfloat16),
        ),
        in_specs=[hbm, vmem, hbm, hbm],
        out_specs=(vmem, vmem),
        scratch_shapes=[
            pltpu.VMEM((members, rows, width), jnp.bfloat16),
            pltpu.VMEM((members,) + note.shape, jnp.float32),
            pltpu.VMEM((members, width, cols), jnp.bfloat16),
            pltpu.VMEM(kvw.shape, jnp.bfloat16),
            pltpu.VMEM((rows, cols), jnp.float32),
            pltpu.VMEM((2, rows, 128), jnp.float32),
            pltpu.VMEM(swap, jnp.bfloat16),
            pltpu.VMEM(swap, jnp.bfloat16),
            pltpu.VMEM((members, PAD, kv_cols), jnp.bfloat16),
            pltpu.VMEM((members, PAD, kv_cols), jnp.bfloat16),
            dma((members,)),
            dma((2,)),
            dma((2, DEPTH, 4)),
            dma((DEPTH, 3)),
            dma((2 * DEPTH,)),
            dma((members, 4)),
            dma((2, members)),
            dma((2, members)),
            dma((2, members)),
        ],
        compiler_params=pltpu.CompilerParams(
            collective_id=0, has_side_effects=True, vmem_limit_bytes=48 * 1024 * 1024
        ),
    )(x, note, wq, kvw)


def output_kernel(
    att_ref,
    x_hbm,
    wo_hbm,
    out_ref,
    att_got,
    att,
    wbuf,
    mine,
    c_send,
    c_got,
    y_send,
    y_got,
    z_send,
    z_got,
    x,
    w_sem,
    x_sem,
    att_sem,
    c_sem,
    y_sem,
    z_sem,
):
    members = att_ref.shape[0]
    rows, width = out_ref.shape
    me, z, y, c = place()
    sibling = slot_of(z, y, 1 - c)
    across = slot_of(z, 1 - y, c)
    above = slot_of(jnp.minimum(z + 1, DEPTH - 1), y, c)
    below = slot_of(jnp.maximum(z - 1, 0), y, c)
    order = far_to_near(z)
    parts = pieces(rows)
    lanes = parts + [pl.ds(rows, FIRST)]
    x_copy = pltpu.make_async_copy(x_hbm, x, x_sem)

    def weights_copy(slot):
        start = pl.multiple_of(slot * width, 128)
        return pltpu.make_async_copy(
            wo_hbm.at[:, pl.ds(start, width)], wbuf.at[slot], w_sem.at[slot]
        )

    for zz in order:
        for yy in (1 - y, y):
            for cc in (1 - c, c):
                weights_copy(slot_of(zz, yy, cc)).start()
    x_copy.start()
    meet_all(members, me)

    def swap(k):
        peer = (me + k) % members
        return peer, att_ref.at[peer], att_sem.at[0, peer]

    for k in range(1, members):
        peer, src, sem = swap(k)
        remote(src, att_got.at[me], sem, att_sem.at[1, me], peer).start()
    att_got[me] = att_ref[me]
    for k in range(1, members):
        peer, src, sem = swap(k)
        remote(src, att_got.at[peer], sem, att_sem.at[1, peer], peer).wait()
    gathered = att_got[...].reshape(members * PAD, att.shape[1])
    att[...] = jnp.dot(
        spread_rows(members, rows, rows // members, True),
        gathered, preferred_element_type=jnp.float32
    ).astype(jnp.bfloat16)

    tile = width // 3 if width % 384 == 0 else width

    def product(slot, store):
        weights_copy(slot).wait()

        def one(t, carry):
            cols = pl.ds(pl.multiple_of(t * tile, 128), tile)
            store(
                cols, jnp.dot(att[...], wbuf[slot, :, cols], preferred_element_type=jnp.float32)
            )
            return carry

        lax.fori_loop(0, width // tile, one, 0)

    def aside(p):
        return remote(c_send.at[p], c_got.at[p], c_sem.at[0, p], c_sem.at[1, p], sibling)

    def over(i, k):
        return remote(
            y_send.at[i, parts[k], :],
            y_got.at[i, parts[k], :],
            y_sem.at[0, i, k],
            y_sem.at[1, i, k],
            across,
        )

    def up(zz, k):
        return remote(
            z_send.at[zz, lanes[k], :],
            z_got.at[0, zz, lanes[k], :],
            z_sem.at[0, zz, k],
            z_sem.at[1, zz, k],
            above,
        )

    def down(zz, k):
        return remote(
            z_send.at[zz, lanes[k], :],
            z_got.at[1, zz, lanes[k], :],
            z_sem.at[0, zz, k],
            z_sem.at[2, zz, k],
            below,
        )

    def add(p, k, ref, *place):
        mine[p, parts[k % 3], :] += ref[(*place, lanes[k], slice(None))].astype(jnp.float32)

    def blocks(i):
        for j, yy in enumerate((1 - y, y)):
            p = 2 * i + j

            def to_sibling(cols, value):
                c_send[p, :, cols] = value.astype(jnp.bfloat16)

            product(slot_of(order[i], yy, 1 - c), to_sibling)
            aside(p).start()
        for j, yy in enumerate((1 - y, y)):
            p = 2 * i + j

            def keep(cols, value):
                mine[p, :, cols] = value

            product(slot_of(order[i], yy, c), keep)
            aside(p).wait_recv()
            mine[p] += c_got[p].astype(jnp.float32)
            if j == 0:
                for k in (1, 2):
                    y_send[i, parts[k], :] = mine[p, parts[k], :].astype(jnp.bfloat16)
                    over(i, k).start()

    def pass_on(i, k):
        zz = order[i]
        p = 2 * i + (0 if k == 3 else 1)

        def send(step):
            z_send[zz, lanes[k], :] = mine[p, parts[k % 3], :].astype(jnp.bfloat16)
            step(zz, k).start()

        @pl.when(zz > z)
        def _():
            @pl.when(z > 0)
            def _():
                up(zz, k).wait_recv()
                add(p, k, z_got, 0, zz)

            send(up)

        @pl.when(zz < z)
        def _():
            @pl.when(z < DEPTH - 1)
            def _():
                down(zz, k).wait_recv()
                add(p, k, z_got, 1, zz)

            send(down)

    def close(k):
        p = 2 * DEPTH - 2 + (0 if k == 3 else 1)

        @pl.when(z > 0)
        def _():
            up(z, k).wait_recv()
            add(p, k, z_got, 0, z)

        @pl.when(z < DEPTH - 1)
        def _():
            down(z, k).wait_recv()
            add(p, k, z_got, 1, z)

    def heads(i):
        pass_on(i, 3)
        pass_on(i, 0)

    def tails(i):
        for k in (1, 2):
            over(i, k).wait_recv()
            add(2 * i + 1, k, y_got, i)
            pass_on(i, k)

    blocks(0)
    blocks(1)
    heads(0)
    blocks(2)
    heads(1)
    tails(0)
    blocks(3)
    heads(2)
    tails(1)
    tails(2)
    last = DEPTH - 1
    close(3)
    y_send[last, parts[0], :] = mine[2 * last, parts[0], :].astype(jnp.bfloat16)
    over(last, 0).start()
    close(0)
    x_copy.wait()
    for k in (1, 2, 0):
        over(last, k).wait_recv()
        add(2 * last + 1, k, y_got, last)
        if k > 0:
            close(k)
        total = x[parts[k], :].astype(jnp.float32) + mine[2 * last + 1, parts[k], :]
        out_ref[parts[k], :] = total.astype(jnp.bfloat16)
    for i in range(DEPTH):
        over(i, 1).wait_send()
        over(i, 2).wait_send()
        aside(2 * i).wait_send()
        aside(2 * i + 1).wait_send()
    over(last, 0).wait_send()
    for i in range(last):
        for k in range(4):
            up(order[i], k).wait_send()


def output_call(att, x, wo, members):
    rows, width = x.shape
    depth = wo.shape[0]
    vmem = pl.BlockSpec(memory_space=pltpu.VMEM)
    dma = pltpu.SemaphoreType.DMA
    hbm = pl.BlockSpec(memory_space=pl.ANY)
    block = (rows, width)
    tall = (rows + FIRST, width)
    return pl.pallas_call(
        output_kernel,
        out_shape=jax.ShapeDtypeStruct(block, jnp.bfloat16),
        in_specs=[vmem, hbm, hbm],
        out_specs=vmem,
        scratch_shapes=[
            pltpu.VMEM(att.shape, jnp.bfloat16),
            pltpu.VMEM((rows, depth), jnp.bfloat16),
            pltpu.VMEM((members, depth, width), jnp.bfloat16),
            pltpu.VMEM((2 * DEPTH,) + block, jnp.float32),
            pltpu.VMEM((2 * DEPTH,) + block, jnp.bfloat16),
            pltpu.VMEM((2 * DEPTH,) + block, jnp.bfloat16),
            pltpu.VMEM((DEPTH,) + block, jnp.bfloat16),
            pltpu.VMEM((DEPTH,) + block, jnp.bfloat16),
            pltpu.VMEM((DEPTH,) + tall, jnp.bfloat16),
            pltpu.VMEM((2, DEPTH) + tall, jnp.bfloat16),
            pltpu.VMEM(block, jnp.bfloat16),
            dma((members,)),
            dma,
            dma((2, members)),
            dma((2, 2 * DEPTH)),
            dma((2, DEPTH, 3)),
            dma((3, DEPTH, 4)),
        ],
        compiler_params=pltpu.CompilerParams(
            collective_id=1, has_side_effects=True, vmem_limit_bytes=56 * 1024 * 1024
        ),
    )(att, x, wo)


def attention(query3, new_entry, cache_entries, cache_lengths):
    head_size = query3.shape[2]
    keys = cache_entries[:, :, :head_size]
    values = cache_entries[:, :, head_size:]
    scores = jnp.einsum("rhd,rld->rhl", query3, keys, preferred_element_type=jnp.float32)
    fresh = jnp.einsum(
        "rhd,rd->rh", query3, new_entry[:, :head_size], preferred_element_type=jnp.float32
    )
    valid = jnp.arange(keys.shape[1])[None, :] < cache_lengths[:, None]
    scores = jnp.where(valid[:, None, :], scores, -1e30)
    peak = jnp.maximum(jnp.max(scores, axis=-1), fresh)
    weights = jnp.exp(scores - peak[..., None]) * valid[:, None, :].astype(jnp.float32)
    fresh_w = jnp.exp(fresh - peak)
    total = jnp.sum(weights, axis=-1) + fresh_w
    probs = (weights / total[..., None]).astype(jnp.bfloat16)
    fresh_p = (fresh_w / total).astype(jnp.bfloat16)
    mixed = jnp.einsum("rhl,rld->rhd", probs, values, preferred_element_type=jnp.float32)
    mixed = mixed + fresh_p.astype(jnp.float32)[..., None] * new_entry[:, None, head_size:].astype(
        jnp.float32
    )
    return mixed.astype(jnp.bfloat16)


def fast_device(
    hidden_state, norm_gain, query_weight, keyval_weight, out_weight, cache_entries, cache_lengths
):
    members = lax.axis_size("gx")
    rows_all, width = hidden_state.shape
    rows = rows_all // members
    head_size = keyval_weight.shape[1] // 2
    cols = query_weight.shape[1]
    state32 = hidden_state.astype(jnp.float32)
    sums = jnp.stack([jnp.sum(state32, axis=1), jnp.sum(state32 * state32, axis=1)])
    sums = jnp.pad(sums, ((0, 0), (0, 256 - rows_all))).reshape(4, 128)
    note = jnp.concatenate([sums, norm_gain.reshape(-1, 128)], axis=0)
    note = jnp.pad(note, ((0, -note.shape[0] % 8), (0, 0)))
    q_rows, kv_rows = query_call(
        hidden_state, note, query_weight, keyval_weight, members, head_size ** (-0.5)
    )
    query3 = q_rows[:, :rows].transpose(1, 0, 2).reshape(rows, -1, head_size)
    mixed = attention(query3, kv_rows[:rows], cache_entries, cache_lengths)
    att = mixed.reshape(rows, members, cols).transpose(1, 0, 2)
    att = jnp.pad(att, ((0, 0), (0, PAD - rows), (0, 0)))
    return output_call(att, hidden_state, out_weight, members)


def on_device(hidden_state, *others):
    members = lax.axis_size("gx")
    rows_all, width = hidden_state.shape
    fits = width % 128 == 0 and 128 < rows_all <= 256 and rows_all % 32 == 0
    if members == 4 * DEPTH and fits and rows_all // members <= PAD:
        return fast_device(hidden_state, *others)
    return plain_device(hidden_state, *others)


def solution(mesh):
    in_specs = (
        P("groups", "gx"),
        P("gx"),
        P(None, "gx"),
        P("gx", None),
        P("gx", None),
        P(("groups", "gx"), None, None),
        P(("groups", "gx")),
    )
    out_specs = P("groups", "gx")
    return jax.shard_map(
        on_device, mesh=mesh, in_specs=in_specs, out_specs=out_specs, check_vma=False
    )
```

```python
import jax
import jax.numpy as jnp
from jax import lax
from jax.experimental import pallas as pl
from jax.experimental.pallas import tpu as pltpu
from jax.sharding import PartitionSpec as P


def plain_device(
    hidden_state, norm_gain, query_weight, keyval_weight, out_weight, cache_entries, cache_lengths
):
    members = lax.axis_size("gx")
    rows_all = hidden_state.shape[0]
    width_local = hidden_state.shape[1]
    width = width_local * members
    rows_local = rows_all // members
    head_size = keyval_weight.shape[1] // 2
    state32 = hidden_state.astype(jnp.float32)
    row_total, row_squares = lax.psum(
        (jnp.sum(state32, axis=1), jnp.sum(state32 * state32, axis=1)), "gx"
    )
    row_mean = row_total / width
    row_var = row_squares / width - row_mean * row_mean
    normed_local = (
        (state32 - row_mean[:, None]) * lax.rsqrt(row_var + 1e-05)[:, None] * norm_gain
    ).astype(jnp.bfloat16)
    query_sum = jnp.dot(
        lax.all_gather(normed_local, "gx", axis=1, tiled=True),
        query_weight,
        preferred_element_type=jnp.float32,
    )
    query = (query_sum * head_size ** (-0.5)).astype(jnp.bfloat16)
    new_entry = lax.psum_scatter(
        jnp.dot(normed_local, keyval_weight, preferred_element_type=jnp.float32).astype(
            jnp.bfloat16
        ),
        "gx",
        scatter_dimension=0,
        tiled=True,
    )
    query_rows = lax.all_to_all(query, "gx", split_axis=0, concat_axis=1, tiled=True)
    heads_all = query_rows.shape[1] // head_size
    query3 = query_rows.reshape(rows_local, heads_all, head_size)
    keys = cache_entries[:, :, :head_size]
    values = cache_entries[:, :, head_size:]
    scores = jnp.einsum("rhd,rld->rhl", query3, keys, preferred_element_type=jnp.float32)
    fresh = jnp.einsum(
        "rhd,rd->rh", query3, new_entry[:, :head_size], preferred_element_type=jnp.float32
    )
    valid = jnp.arange(keys.shape[1])[None, :] < cache_lengths[:, None]
    scores = jnp.where(valid[:, None, :], scores, -1e30)
    peak = jnp.maximum(jnp.max(scores, axis=-1), fresh)
    weights = jnp.exp(scores - peak[..., None]) * valid[:, None, :].astype(jnp.float32)
    fresh_w = jnp.exp(fresh - peak)
    total = jnp.sum(weights, axis=-1) + fresh_w
    probs = (weights / total[..., None]).astype(jnp.bfloat16)
    fresh_p = (fresh_w / total).astype(jnp.bfloat16)
    mixed = jnp.einsum("rhl,rld->rhd", probs, values, preferred_element_type=jnp.float32)
    mixed = mixed + fresh_p.astype(jnp.float32)[..., None] * new_entry[:, None, head_size:].astype(
        jnp.float32
    )
    attended_rows = mixed.reshape(rows_local, heads_all * head_size).astype(jnp.bfloat16)
    attended = lax.all_to_all(attended_rows, "gx", split_axis=1, concat_axis=0, tiled=True)
    partial_out = jnp.dot(attended, out_weight, preferred_element_type=jnp.float32)
    summed = lax.psum_scatter(
        partial_out.astype(jnp.bfloat16), "gx", scatter_dimension=1, tiled=True
    ).astype(jnp.float32)
    return (hidden_state.astype(jnp.float32) + summed).astype(jnp.bfloat16)


MESH = pl.DeviceIdType.MESH
PAD = 16
DEPTH = 4
FIRST = 32


def remote(src, dst, send, recv, peer):
    return pltpu.make_async_remote_copy(
        src_ref=src,
        dst_ref=dst,
        send_sem=send,
        recv_sem=recv,
        device_id={"gx": peer},
        device_id_type=MESH,
    )


def meet_all(members, me):
    barrier = pltpu.get_barrier_semaphore()
    for k in range(1, members):
        pl.semaphore_signal(
            barrier, inc=1, device_id={"gx": (me + k) % members}, device_id_type=MESH
        )
    pl.semaphore_wait(barrier, members - 1)


def place():
    me = lax.axis_index("gx")
    return me, me // 4, (me // 2) % 2, me % 2


def far_to_near(z):
    first = 3 * (1 - z // 2)
    third = 1 + z % 2
    return [first, 6 - z - first - third, third, z]


def pieces(rows):
    half = (rows - FIRST) // 2
    return [pl.ds(0, FIRST), pl.ds(FIRST, half), pl.ds(FIRST + half, half)]


def spread_rows(members, rows, local, flip):
    shape = (rows, members * PAD) if flip else (members * PAD, rows)
    p = lax.broadcasted_iota(jnp.int32, shape, 1 if flip else 0)
    r = lax.broadcasted_iota(jnp.int32, shape, 0 if flip else 1)
    inner = p & (PAD - 1)
    hit = (inner < local) & ((p >> 4) * local + inner == r)
    return jnp.where(hit, 1.0, 0.0).astype(jnp.bfloat16)


def slot_of(z, y, c):
    return z * 4 + y * 2 + c


def query_kernel(
    head_scale,
    x_hbm,
    note_ref,
    wq_hbm,
    kvw_hbm,
    cache_hbm,
    lengths,
    att_out,
    buf,
    notes,
    wbuf,
    kvw,
    cache,
    att_rows,
    acc,
    stat,
    q_send,
    q_got,
    kv_send,
    kv_got,
    w_sem,
    own_sem,
    z_sem,
    y_sem,
    c_sem,
    recv_sem,
    note_sem,
    kv_sem,
    q_sem,
):
    members = buf.shape[0]
    rows, width = x_hbm.shape
    parts = pieces(rows)
    total_width = width * members
    me, z, y, c = place()
    sibling = slot_of(z, y, 1 - c)
    across = slot_of(z, 1 - y, c)
    above = slot_of(jnp.minimum(z + 1, DEPTH - 1), y, c)
    below = slot_of(jnp.maximum(z - 1, 0), y, c)

    def weights_copy(slot):
        start = pl.multiple_of(slot * width, 128)
        return pltpu.make_async_copy(
            wq_hbm.at[pl.ds(start, width), :], wbuf.at[slot], w_sem.at[slot]
        )

    own = pltpu.make_async_copy(x_hbm, buf.at[me], own_sem.at[0])
    own.start()
    kvw_copy = pltpu.make_async_copy(kvw_hbm, kvw, own_sem.at[1])
    kvw_copy.start()
    cache_copy = pltpu.make_async_copy(cache_hbm, cache, own_sem.at[2])
    notes[me] = note_ref[...]
    order = far_to_near(z)[::-1]
    own.wait()
    meet_all(members, me)

    def shard(slot, piece, send, peer):
        rows_of = pl.ds(0, rows) if piece == 3 else parts[piece]
        block = buf.at[slot, rows_of, :]
        return remote(block, block, send, recv_sem.at[slot, piece], peer)

    def up(zz, k):
        yy = 1 - y if k == 3 else y
        return shard(slot_of(zz, yy, c), k % 3, z_sem.at[0, zz, k], above)

    def down(zz, k):
        yy = 1 - y if k == 3 else y
        return shard(slot_of(zz, yy, c), k % 3, z_sem.at[1, zz, k], below)

    def over(zz, k):
        return shard(slot_of(zz, y, c), k, y_sem.at[zz, k], across)

    def aside(zz, yy):
        return shard(slot_of(zz, yy, c), 3, c_sem.at[zz * 2 + yy], sibling)

    def arrived(slot, piece):
        shard(slot, piece, own_sem.at[0], sibling).wait_recv()

    def both_ways(k):
        @pl.when(z < DEPTH - 1)
        def _():
            up(z, k).start()

        @pl.when(z > 0)
        def _():
            down(z, k).start()

    def relay(i, k):
        yy = 1 - y if k == 3 else y

        @pl.when(z - i >= 0)
        def _():
            low = jnp.maximum(z - i, 0)
            arrived(slot_of(low, yy, c), k % 3)

            @pl.when(z < DEPTH - 1)
            def _():
                up(low, k).start()

        @pl.when(z + i < DEPTH)
        def _():
            high = jnp.minimum(z + i, DEPTH - 1)
            arrived(slot_of(high, yy, c), k % 3)

            @pl.when(z > 0)
            def _():
                down(high, k).start()

    def spread(src_of, dst, sems):
        for k in range(1, members):
            peer = (me + k) % members
            remote(src_of(peer), dst.at[me], sems.at[0, peer], sems.at[1, me], peer).start()

    def collect(src_of, dst, sems):
        for k in range(1, members):
            peer = (me + k) % members
            remote(src_of(peer), dst.at[peer], sems.at[0, peer], sems.at[1, peer], peer).wait()

    spread(lambda peer: note_ref, notes, note_sem)
    over(z, 0).start()
    both_ways(1)
    over(z, 1).start()
    both_ways(2)
    over(z, 2).start()
    both_ways(0)
    aside(z, y).start()
    for slot in range(members):
        weights_copy(slot).start()
    cache_copy.start()
    collect(lambda peer: note_ref, notes, note_sem)

    mean = jnp.sum(notes[:, 0:2, :], axis=0) / total_width
    var = jnp.sum(notes[:, 2:4, :], axis=0) / total_width - mean * mean
    inv = lax.rsqrt(var + 1e-05)
    stat[0, 0:128, :] = jnp.broadcast_to(mean[0:1, :], (128, 128)).T
    stat[1, 0:128, :] = jnp.broadcast_to(inv[0:1, :], (128, 128)).T
    stat[0, 128:rows, :] = jnp.broadcast_to(mean[1:2, :], (128, 128)).T[0 : rows - 128]
    stat[1, 128:rows, :] = jnp.broadcast_to(inv[1:2, :], (128, 128)).T[0 : rows - 128]

    def normed(slot):
        tiles = []
        for t in range(width // 128):
            part = buf[slot, :, t * 128 : (t + 1) * 128].astype(jnp.float32)
            gain = notes[slot, 4 + t : 5 + t, :]
            tiles.append(((part - stat[0]) * stat[1] * gain).astype(jnp.bfloat16))
        return jnp.concatenate(tiles, axis=1)

    arrived(slot_of(z, 1 - y, c), 0)
    both_ways(3)
    kvw_copy.wait()
    select = spread_rows(members, rows, rows // members, False)
    kv = jnp.dot(normed(me), kvw[...], preferred_element_type=jnp.float32)
    kv = jnp.dot(select, kv.astype(jnp.bfloat16), preferred_element_type=jnp.float32)
    kv_send[...] = kv.astype(jnp.bfloat16).reshape(kv_send.shape)
    spread(lambda peer: kv_send.at[peer], kv_got, kv_sem)
    kv_got[me] = kv_send[me]
    acc[...] = jnp.zeros_like(acc)

    def work(zz, yy):
        def one(k, carry):
            slot = slot_of(zz, yy, (c + k) % 2)

            @pl.when(k == 1)
            def _():
                arrived(slot, 3)

            weights_copy(slot).wait()
            acc[...] += jnp.dot(normed(slot), wbuf[slot], preferred_element_type=jnp.float32)
            return carry

        lax.fori_loop(0, 2, one, 0)

    def finish_across(i):
        slot = slot_of(order[i], 1 - y, c)
        arrived(slot, 1)
        arrived(slot, 2)
        aside(order[i], 1 - y).start()

    for i in range(1, DEPTH):
        relay(i, 1)
        over(order[i], 1).start()
        work(order[i - 1], y)
        relay(i, 2)
        over(order[i], 2).start()
        finish_across(i - 1)
        relay(i, 0)
        aside(order[i], y).start()
        relay(i, 3)
        work(order[i - 1], 1 - y)
    work(order[DEPTH - 1], y)
    finish_across(DEPTH - 1)
    work(order[DEPTH - 1], 1 - y)

    query = (acc[...] * head_scale).astype(jnp.bfloat16)
    query = jnp.dot(select, query, preferred_element_type=jnp.float32)
    q_send[...] = query.astype(jnp.bfloat16).reshape(q_send.shape)
    spread(lambda peer: q_send.at[peer], q_got, q_sem)
    q_got[me] = q_send[me]
    collect(lambda peer: kv_send.at[peer], kv_got, kv_sem)
    fresh_kv = jnp.sum(kv_got[...].astype(jnp.float32), axis=0).astype(jnp.bfloat16)
    fresh_kv = fresh_kv.astype(jnp.float32)
    cache_copy.wait()
    for zz in range(DEPTH):
        for piece in range(3):
            over_sent = (piece > 0) | (zz == z)

            @pl.when(over_sent)
            def _():
                over(zz, piece).wait_send()

        aside(zz, 0).wait_send()
        aside(zz, 1).wait_send()

        @pl.when((z < DEPTH - 1) & (zz <= z))
        def _():
            for piece in range(4):
                up(zz, piece).wait_send()

        @pl.when((z > 0) & (zz >= z))
        def _():
            for piece in range(4):
                down(zz, piece).wait_send()

    collect(lambda peer: q_send.at[peer], q_got, q_sem)
    shape = (members * PAD, members * PAD)
    to = lax.broadcasted_iota(jnp.int32, shape, 0)
    of = lax.broadcasted_iota(jnp.int32, shape, 1)
    turn = ((to & (PAD - 1)) * PAD + (to >> 4)) == of
    turn = jnp.where(turn, 1.0, 0.0).astype(jnp.bfloat16)
    flat = q_got[...].reshape(members * PAD, q_got.shape[2])
    by_row = jnp.dot(turn, flat, preferred_element_type=jnp.float32)
    local = rows // members
    head = cache.shape[2] // 2
    att_rows[...] = jnp.zeros_like(att_rows)
    for r in range(local):
        span = slice(r * PAD, (r + 1) * PAD)
        q32 = jnp.concatenate([by_row[span, 0:head], by_row[span, head : 2 * head]], axis=0)
        scores = lax.dot_general(
            q32.astype(jnp.bfloat16),
            cache[r, :, 0:head],
            (((1,), (1,)), ((), ())),
            preferred_element_type=jnp.float32,
        )
        fresh = jnp.sum(q32 * fresh_kv[r : r + 1, 0:head], axis=1, keepdims=True)
        slots = lax.broadcasted_iota(jnp.int32, scores.shape, 1)
        valid = slots < lengths[r]
        scores = jnp.where(valid, scores, -1e30)
        peak = jnp.maximum(jnp.max(scores, axis=1, keepdims=True), fresh)
        weights = jnp.where(valid, jnp.exp(scores - peak), 0.0)
        fresh_w = jnp.exp(fresh - peak)
        total = jnp.sum(weights, axis=1, keepdims=True) + fresh_w
        probs = (weights / total).astype(jnp.bfloat16)
        fresh_p = (fresh_w / total).astype(jnp.bfloat16).astype(jnp.float32)
        mixed = jnp.dot(probs, cache[r, :, head : 2 * head], preferred_element_type=jnp.float32)
        mixed = (mixed + fresh_p * fresh_kv[r : r + 1, head : 2 * head]).astype(jnp.bfloat16)
        att_rows[span, 0:head] = mixed[0:PAD]
        att_rows[span, head : 2 * head] = mixed[PAD : 2 * PAD]
    back = jnp.dot(turn, att_rows[...], preferred_element_type=jnp.float32)
    att_out[...] = back.astype(jnp.bfloat16).reshape(att_out.shape)


def query_call(x, note, wq, kvw, cache, lengths, members, head_scale):
    rows, width = x.shape
    cols = wq.shape[1]
    vmem = pl.BlockSpec(memory_space=pltpu.VMEM)
    hbm = pl.BlockSpec(memory_space=pl.ANY)
    swap = (members, PAD, cols)
    kv_cols = kvw.shape[1]
    dma = pltpu.SemaphoreType.DMA
    return pl.pallas_call(
        lambda *refs: query_kernel(head_scale, *refs),
        out_shape=jax.ShapeDtypeStruct(swap, jnp.bfloat16),
        in_specs=[hbm, vmem, hbm, hbm, hbm, pl.BlockSpec(memory_space=pltpu.SMEM)],
        out_specs=vmem,
        scratch_shapes=[
            pltpu.VMEM((members, rows, width), jnp.bfloat16),
            pltpu.VMEM((members,) + note.shape, jnp.float32),
            pltpu.VMEM((members, width, cols), jnp.bfloat16),
            pltpu.VMEM(kvw.shape, jnp.bfloat16),
            pltpu.VMEM(cache.shape, jnp.bfloat16),
            pltpu.VMEM((members * PAD, cols), jnp.bfloat16),
            pltpu.VMEM((rows, cols), jnp.float32),
            pltpu.VMEM((2, rows, 128), jnp.float32),
            pltpu.VMEM(swap, jnp.bfloat16),
            pltpu.VMEM(swap, jnp.bfloat16),
            pltpu.VMEM((members, PAD, kv_cols), jnp.bfloat16),
            pltpu.VMEM((members, PAD, kv_cols), jnp.bfloat16),
            dma((members,)),
            dma((3,)),
            dma((2, DEPTH, 4)),
            dma((DEPTH, 3)),
            dma((2 * DEPTH,)),
            dma((members, 4)),
            dma((2, members)),
            dma((2, members)),
            dma((2, members)),
        ],
        compiler_params=pltpu.CompilerParams(
            collective_id=0, has_side_effects=True, vmem_limit_bytes=60 * 1024 * 1024
        ),
    )(x, note, wq, kvw, cache, lengths)


def output_kernel(
    att_ref,
    x_hbm,
    wo_hbm,
    out_ref,
    att_got,
    att,
    wbuf,
    mine,
    c_send,
    c_got,
    y_send,
    y_got,
    z_send,
    z_got,
    x,
    w_sem,
    x_sem,
    att_sem,
    c_sem,
    y_sem,
    z_sem,
):
    members = att_ref.shape[0]
    rows, width = out_ref.shape
    me, z, y, c = place()
    sibling = slot_of(z, y, 1 - c)
    across = slot_of(z, 1 - y, c)
    above = slot_of(jnp.minimum(z + 1, DEPTH - 1), y, c)
    below = slot_of(jnp.maximum(z - 1, 0), y, c)
    order = far_to_near(z)
    parts = pieces(rows)
    lanes = parts + [pl.ds(rows, FIRST)]
    x_copy = pltpu.make_async_copy(x_hbm, x, x_sem)

    def weights_copy(slot):
        start = pl.multiple_of(slot * width, 128)
        return pltpu.make_async_copy(
            wo_hbm.at[:, pl.ds(start, width)], wbuf.at[slot], w_sem.at[slot]
        )

    for zz in order:
        for yy in (1 - y, y):
            for cc in (1 - c, c):
                weights_copy(slot_of(zz, yy, cc)).start()
    x_copy.start()
    meet_all(members, me)

    def swap(k):
        peer = (me + k) % members
        return peer, att_ref.at[peer], att_sem.at[0, peer]

    for k in range(1, members):
        peer, src, sem = swap(k)
        remote(src, att_got.at[me], sem, att_sem.at[1, me], peer).start()
    att_got[me] = att_ref[me]
    for k in range(1, members):
        peer, src, sem = swap(k)
        remote(src, att_got.at[peer], sem, att_sem.at[1, peer], peer).wait()
    gathered = att_got[...].reshape(members * PAD, att.shape[1])
    att[...] = jnp.dot(
        spread_rows(members, rows, rows // members, True),
        gathered, preferred_element_type=jnp.float32
    ).astype(jnp.bfloat16)

    tile = width // 3 if width % 384 == 0 else width

    def product(slot, store):
        weights_copy(slot).wait()

        def one(t, carry):
            cols = pl.ds(pl.multiple_of(t * tile, 128), tile)
            store(
                cols, jnp.dot(att[...], wbuf[slot, :, cols], preferred_element_type=jnp.float32)
            )
            return carry

        lax.fori_loop(0, width // tile, one, 0)

    def aside(p):
        return remote(c_send.at[p], c_got.at[p], c_sem.at[0, p], c_sem.at[1, p], sibling)

    def over(i, k):
        return remote(
            y_send.at[i, parts[k], :],
            y_got.at[i, parts[k], :],
            y_sem.at[0, i, k],
            y_sem.at[1, i, k],
            across,
        )

    def up(zz, k):
        return remote(
            z_send.at[zz, lanes[k], :],
            z_got.at[0, zz, lanes[k], :],
            z_sem.at[0, zz, k],
            z_sem.at[1, zz, k],
            above,
        )

    def down(zz, k):
        return remote(
            z_send.at[zz, lanes[k], :],
            z_got.at[1, zz, lanes[k], :],
            z_sem.at[0, zz, k],
            z_sem.at[2, zz, k],
            below,
        )

    def add(p, k, ref, *place):
        mine[p, parts[k % 3], :] += ref[(*place, lanes[k], slice(None))].astype(jnp.float32)

    def blocks(i):
        for j, yy in enumerate((1 - y, y)):
            p = 2 * i + j

            def to_sibling(cols, value):
                c_send[p, :, cols] = value.astype(jnp.bfloat16)

            product(slot_of(order[i], yy, 1 - c), to_sibling)
            aside(p).start()
        for j, yy in enumerate((1 - y, y)):
            p = 2 * i + j

            def keep(cols, value):
                mine[p, :, cols] = value

            product(slot_of(order[i], yy, c), keep)
            aside(p).wait_recv()
            mine[p] += c_got[p].astype(jnp.float32)
            if j == 0:
                for k in (1, 2):
                    y_send[i, parts[k], :] = mine[p, parts[k], :].astype(jnp.bfloat16)
                    over(i, k).start()

    def pass_on(i, k):
        zz = order[i]
        p = 2 * i + (0 if k == 3 else 1)

        def send(step):
            z_send[zz, lanes[k], :] = mine[p, parts[k % 3], :].astype(jnp.bfloat16)
            step(zz, k).start()

        @pl.when(zz > z)
        def _():
            @pl.when(z > 0)
            def _():
                up(zz, k).wait_recv()
                add(p, k, z_got, 0, zz)

            send(up)

        @pl.when(zz < z)
        def _():
            @pl.when(z < DEPTH - 1)
            def _():
                down(zz, k).wait_recv()
                add(p, k, z_got, 1, zz)

            send(down)

    def close(k):
        p = 2 * DEPTH - 2 + (0 if k == 3 else 1)

        @pl.when(z > 0)
        def _():
            up(z, k).wait_recv()
            add(p, k, z_got, 0, z)

        @pl.when(z < DEPTH - 1)
        def _():
            down(z, k).wait_recv()
            add(p, k, z_got, 1, z)

    def heads(i):
        pass_on(i, 3)
        pass_on(i, 0)

    def tails(i):
        for k in (1, 2):
            over(i, k).wait_recv()
            add(2 * i + 1, k, y_got, i)
            pass_on(i, k)

    blocks(0)
    blocks(1)
    heads(0)
    blocks(2)
    heads(1)
    tails(0)
    blocks(3)
    heads(2)
    tails(1)
    tails(2)
    last = DEPTH - 1
    close(3)
    y_send[last, parts[0], :] = mine[2 * last, parts[0], :].astype(jnp.bfloat16)
    over(last, 0).start()
    close(0)
    x_copy.wait()
    for k in (1, 2, 0):
        over(last, k).wait_recv()
        add(2 * last + 1, k, y_got, last)
        if k > 0:
            close(k)
        total = x[parts[k], :].astype(jnp.float32) + mine[2 * last + 1, parts[k], :]
        out_ref[parts[k], :] = total.astype(jnp.bfloat16)
    for i in range(DEPTH):
        over(i, 1).wait_send()
        over(i, 2).wait_send()
        aside(2 * i).wait_send()
        aside(2 * i + 1).wait_send()
    over(last, 0).wait_send()
    for i in range(last):
        for k in range(4):
            up(order[i], k).wait_send()


def output_call(att, x, wo, members):
    rows, width = x.shape
    depth = wo.shape[0]
    vmem = pl.BlockSpec(memory_space=pltpu.VMEM)
    dma = pltpu.SemaphoreType.DMA
    hbm = pl.BlockSpec(memory_space=pl.ANY)
    block = (rows, width)
    tall = (rows + FIRST, width)
    return pl.pallas_call(
        output_kernel,
        out_shape=jax.ShapeDtypeStruct(block, jnp.bfloat16),
        in_specs=[vmem, hbm, hbm],
        out_specs=vmem,
        scratch_shapes=[
            pltpu.VMEM(att.shape, jnp.bfloat16),
            pltpu.VMEM((rows, depth), jnp.bfloat16),
            pltpu.VMEM((members, depth, width), jnp.bfloat16),
            pltpu.VMEM((2 * DEPTH,) + block, jnp.float32),
            pltpu.VMEM((2 * DEPTH,) + block, jnp.bfloat16),
            pltpu.VMEM((2 * DEPTH,) + block, jnp.bfloat16),
            pltpu.VMEM((DEPTH,) + block, jnp.bfloat16),
            pltpu.VMEM((DEPTH,) + block, jnp.bfloat16),
            pltpu.VMEM((DEPTH,) + tall, jnp.bfloat16),
            pltpu.VMEM((2, DEPTH) + tall, jnp.bfloat16),
            pltpu.VMEM(block, jnp.bfloat16),
            dma((members,)),
            dma,
            dma((2, members)),
            dma((2, 2 * DEPTH)),
            dma((2, DEPTH, 3)),
            dma((3, DEPTH, 4)),
        ],
        compiler_params=pltpu.CompilerParams(
            collective_id=1, has_side_effects=True, vmem_limit_bytes=60 * 1024 * 1024
        ),
    )(att, x, wo)


def fast_device(
    hidden_state, norm_gain, query_weight, keyval_weight, out_weight, cache_entries, cache_lengths
):
    members = lax.axis_size("gx")
    rows_all, width = hidden_state.shape
    head_size = keyval_weight.shape[1] // 2
    state32 = hidden_state.astype(jnp.float32)
    sums = jnp.stack([jnp.sum(state32, axis=1), jnp.sum(state32 * state32, axis=1)])
    sums = jnp.pad(sums, ((0, 0), (0, 256 - rows_all))).reshape(4, 128)
    note = jnp.concatenate([sums, norm_gain.reshape(-1, 128)], axis=0)
    note = jnp.pad(note, ((0, -note.shape[0] % 8), (0, 0)))
    att = query_call(
        hidden_state,
        note,
        query_weight,
        keyval_weight,
        cache_entries,
        cache_lengths,
        members,
        head_size ** (-0.5),
    )
    return output_call(att, hidden_state, out_weight, members)


def on_device(hidden_state, *others):
    members = lax.axis_size("gx")
    rows_all, width = hidden_state.shape
    fits = width % 128 == 0 and 128 < rows_all <= 256 and rows_all % 32 == 0
    paired = others[1].shape[1] == others[2].shape[1] and members == PAD
    if members == 4 * DEPTH and fits and paired and rows_all // members <= PAD:
        return fast_device(hidden_state, *others)
    return plain_device(hidden_state, *others)


def solution(mesh):
    in_specs = (
        P("groups", "gx"),
        P("gx"),
        P(None, "gx"),
        P("gx", None),
        P("gx", None),
        P(("groups", "gx"), None, None),
        P(("groups", "gx")),
    )
    out_specs = P("groups", "gx")
    return jax.shard_map(
        on_device, mesh=mesh, in_specs=in_specs, out_specs=out_specs, check_vma=False
    )
```

```python
import jax
import jax.numpy as jnp
from jax import lax
from jax.experimental import pallas as pl
from jax.experimental.pallas import tpu as pltpu
from jax.sharding import PartitionSpec as P


def plain_device(
    hidden_state, norm_gain, query_weight, keyval_weight, out_weight, cache_entries, cache_lengths
):
    members = lax.axis_size("gx")
    rows_all = hidden_state.shape[0]
    width_local = hidden_state.shape[1]
    width = width_local * members
    rows_local = rows_all // members
    head_size = keyval_weight.shape[1] // 2
    state32 = hidden_state.astype(jnp.float32)
    row_total, row_squares = lax.psum(
        (jnp.sum(state32, axis=1), jnp.sum(state32 * state32, axis=1)), "gx"
    )
    row_mean = row_total / width
    row_var = row_squares / width - row_mean * row_mean
    normed_local = (
        (state32 - row_mean[:, None]) * lax.rsqrt(row_var + 1e-05)[:, None] * norm_gain
    ).astype(jnp.bfloat16)
    query_sum = jnp.dot(
        lax.all_gather(normed_local, "gx", axis=1, tiled=True),
        query_weight,
        preferred_element_type=jnp.float32,
    )
    query = (query_sum * head_size ** (-0.5)).astype(jnp.bfloat16)
    new_entry = lax.psum_scatter(
        jnp.dot(normed_local, keyval_weight, preferred_element_type=jnp.float32).astype(
            jnp.bfloat16
        ),
        "gx",
        scatter_dimension=0,
        tiled=True,
    )
    query_rows = lax.all_to_all(query, "gx", split_axis=0, concat_axis=1, tiled=True)
    heads_all = query_rows.shape[1] // head_size
    query3 = query_rows.reshape(rows_local, heads_all, head_size)
    keys = cache_entries[:, :, :head_size]
    values = cache_entries[:, :, head_size:]
    scores = jnp.einsum("rhd,rld->rhl", query3, keys, preferred_element_type=jnp.float32)
    fresh = jnp.einsum(
        "rhd,rd->rh", query3, new_entry[:, :head_size], preferred_element_type=jnp.float32
    )
    valid = jnp.arange(keys.shape[1])[None, :] < cache_lengths[:, None]
    scores = jnp.where(valid[:, None, :], scores, -1e30)
    peak = jnp.maximum(jnp.max(scores, axis=-1), fresh)
    weights = jnp.exp(scores - peak[..., None]) * valid[:, None, :].astype(jnp.float32)
    fresh_w = jnp.exp(fresh - peak)
    total = jnp.sum(weights, axis=-1) + fresh_w
    probs = (weights / total[..., None]).astype(jnp.bfloat16)
    fresh_p = (fresh_w / total).astype(jnp.bfloat16)
    mixed = jnp.einsum("rhl,rld->rhd", probs, values, preferred_element_type=jnp.float32)
    mixed = mixed + fresh_p.astype(jnp.float32)[..., None] * new_entry[:, None, head_size:].astype(
        jnp.float32
    )
    attended_rows = mixed.reshape(rows_local, heads_all * head_size).astype(jnp.bfloat16)
    attended = lax.all_to_all(attended_rows, "gx", split_axis=1, concat_axis=0, tiled=True)
    partial_out = jnp.dot(attended, out_weight, preferred_element_type=jnp.float32)
    summed = lax.psum_scatter(
        partial_out.astype(jnp.bfloat16), "gx", scatter_dimension=1, tiled=True
    ).astype(jnp.float32)
    return (hidden_state.astype(jnp.float32) + summed).astype(jnp.bfloat16)


MESH = pl.DeviceIdType.MESH
PAD = 16
DEPTH = 4
FIRST = 32


def remote(src, dst, send, recv, peer):
    return pltpu.make_async_remote_copy(
        src_ref=src,
        dst_ref=dst,
        send_sem=send,
        recv_sem=recv,
        device_id={"gx": peer},
        device_id_type=MESH,
    )


def meet_all(members, me):
    barrier = pltpu.get_barrier_semaphore()
    for k in range(1, members):
        pl.semaphore_signal(
            barrier, inc=1, device_id={"gx": (me + k) % members}, device_id_type=MESH
        )
    pl.semaphore_wait(barrier, members - 1)


def place():
    me = lax.axis_index("gx")
    return me, me // 4, (me // 2) % 2, me % 2


def far_to_near(z):
    first = 3 * (1 - z // 2)
    third = 1 + z % 2
    return [first, 6 - z - first - third, third, z]


def pieces(rows):
    half = (rows - FIRST) // 2
    return [pl.ds(0, FIRST), pl.ds(FIRST, half), pl.ds(FIRST + half, half)]


def spread_rows(members, rows, local, flip):
    shape = (rows, members * PAD) if flip else (members * PAD, rows)
    p = lax.broadcasted_iota(jnp.int32, shape, 1 if flip else 0)
    r = lax.broadcasted_iota(jnp.int32, shape, 0 if flip else 1)
    inner = p & (PAD - 1)
    hit = (inner < local) & ((p >> 4) * local + inner == r)
    return jnp.where(hit, 1.0, 0.0).astype(jnp.bfloat16)


def slot_of(z, y, c):
    return z * 4 + y * 2 + c


def query_kernel(
    head_scale,
    x_hbm,
    note_ref,
    wq_hbm,
    kvw_hbm,
    cache_hbm,
    lengths,
    att_out,
    buf,
    notes,
    wbuf,
    kvw,
    cache,
    att_rows,
    acc,
    stat,
    q_send,
    q_got,
    kv_send,
    kv_got,
    kv_pair,
    w_sem,
    own_sem,
    z_sem,
    y_sem,
    c_sem,
    recv_sem,
    note_sem,
    kv_sem,
    q_sem,
    pair_sem,
):
    members = buf.shape[0]
    rows, width = x_hbm.shape
    parts = pieces(rows)
    total_width = width * members
    me, z, y, c = place()
    sibling = slot_of(z, y, 1 - c)
    across = slot_of(z, 1 - y, c)
    above = slot_of(jnp.minimum(z + 1, DEPTH - 1), y, c)
    below = slot_of(jnp.maximum(z - 1, 0), y, c)

    def weights_copy(slot):
        start = pl.multiple_of(slot * width, 128)
        return pltpu.make_async_copy(
            wq_hbm.at[pl.ds(start, width), :], wbuf.at[slot], w_sem.at[slot]
        )

    own = pltpu.make_async_copy(x_hbm, buf.at[me], own_sem.at[0])
    own.start()
    kvw_copy = pltpu.make_async_copy(kvw_hbm, kvw, own_sem.at[1])
    kvw_copy.start()
    cache_copy = pltpu.make_async_copy(cache_hbm, cache, own_sem.at[2])
    notes[me] = note_ref[...]
    order = far_to_near(z)[::-1]
    own.wait()
    meet_all(members, me)

    def shard(slot, piece, send, peer):
        rows_of = pl.ds(0, rows) if piece == 3 else parts[piece]
        block = buf.at[slot, rows_of, :]
        return remote(block, block, send, recv_sem.at[slot, piece], peer)

    def up(zz, k):
        yy = 1 - y if k == 3 else y
        return shard(slot_of(zz, yy, c), k % 3, z_sem.at[0, zz, k], above)

    def down(zz, k):
        yy = 1 - y if k == 3 else y
        return shard(slot_of(zz, yy, c), k % 3, z_sem.at[1, zz, k], below)

    def over(zz, k):
        return shard(slot_of(zz, y, c), k, y_sem.at[zz, k], across)

    def aside(zz, yy):
        return shard(slot_of(zz, yy, c), 3, c_sem.at[zz * 2 + yy], sibling)

    def arrived(slot, piece):
        shard(slot, piece, own_sem.at[0], sibling).wait_recv()

    def both_ways(k):
        @pl.when(z < DEPTH - 1)
        def _():
            up(z, k).start()

        @pl.when(z > 0)
        def _():
            down(z, k).start()

    def relay(i, k):
        yy = 1 - y if k == 3 else y

        @pl.when(z - i >= 0)
        def _():
            low = jnp.maximum(z - i, 0)
            arrived(slot_of(low, yy, c), k % 3)

            @pl.when(z < DEPTH - 1)
            def _():
                up(low, k).start()

        @pl.when(z + i < DEPTH)
        def _():
            high = jnp.minimum(z + i, DEPTH - 1)
            arrived(slot_of(high, yy, c), k % 3)

            @pl.when(z > 0)
            def _():
                down(high, k).start()

    def spread(src_of, dst, sems):
        for k in range(1, members):
            peer = (me + k) % members
            remote(src_of(peer), dst.at[me], sems.at[0, peer], sems.at[1, me], peer).start()

    def collect(src_of, dst, sems):
        for k in range(1, members):
            peer = (me + k) % members
            remote(src_of(peer), dst.at[peer], sems.at[0, peer], sems.at[1, peer], peer).wait()

    spread(lambda peer: note_ref, notes, note_sem)
    over(z, 0).start()
    both_ways(1)
    over(z, 1).start()
    both_ways(2)
    over(z, 2).start()
    both_ways(0)
    aside(z, y).start()
    for slot in range(members):
        weights_copy(slot).start()
    cache_copy.start()
    collect(lambda peer: note_ref, notes, note_sem)

    mean = jnp.sum(notes[:, 0:2, :], axis=0) / total_width
    var = jnp.sum(notes[:, 2:4, :], axis=0) / total_width - mean * mean
    inv = lax.rsqrt(var + 1e-05)
    stat[0, 0:128, :] = jnp.broadcast_to(mean[0:1, :], (128, 128)).T
    stat[1, 0:128, :] = jnp.broadcast_to(inv[0:1, :], (128, 128)).T
    stat[0, 128:rows, :] = jnp.broadcast_to(mean[1:2, :], (128, 128)).T[0 : rows - 128]
    stat[1, 128:rows, :] = jnp.broadcast_to(inv[1:2, :], (128, 128)).T[0 : rows - 128]

    def normed(slot):
        tiles = []
        for t in range(width // 128):
            part = buf[slot, :, t * 128 : (t + 1) * 128].astype(jnp.float32)
            gain = notes[slot, 4 + t : 5 + t, :]
            tiles.append(((part - stat[0]) * stat[1] * gain).astype(jnp.bfloat16))
        return jnp.concatenate(tiles, axis=1)

    arrived(slot_of(z, 1 - y, c), 0)
    both_ways(3)
    kvw_copy.wait()
    select = spread_rows(members, rows, rows // members, False)
    kv = jnp.dot(normed(me), kvw[...], preferred_element_type=jnp.float32)
    kv = jnp.dot(select, kv.astype(jnp.bfloat16), preferred_element_type=jnp.float32)
    kv_send[...] = kv.astype(jnp.bfloat16).reshape(kv_send.shape)

    def to_pair(k, theirs):
        return remote(
            kv_send.at[2 * k + theirs], kv_pair.at[k], pair_sem.at[0, k], pair_sem.at[1, k], sibling
        )

    def to_owner(k, slot):
        peer = (me + 2 * k) % members
        return remote(
            kv_send.at[peer], kv_got.at[slot], kv_sem.at[0, peer], kv_sem.at[1, slot], peer
        )

    for k in range(members // 2):
        to_pair(k, 1 - c).start()
    for k in range(members // 2):
        to_pair(k, 1 - c).wait()
        pair = kv_send[2 * k + c].astype(jnp.float32) + kv_pair[k].astype(jnp.float32)
        kv_send[2 * k + c] = pair.astype(jnp.bfloat16)
    for k in range(1, members // 2):
        to_owner(k, me // 2).start()
    kv_got[me // 2] = kv_send[me]
    acc[...] = jnp.zeros_like(acc)

    def work(zz, yy):
        def one(k, carry):
            slot = slot_of(zz, yy, (c + k) % 2)

            @pl.when(k == 1)
            def _():
                arrived(slot, 3)

            weights_copy(slot).wait()
            acc[...] += jnp.dot(normed(slot), wbuf[slot], preferred_element_type=jnp.float32)
            return carry

        lax.fori_loop(0, 2, one, 0)

    def finish_across(i):
        slot = slot_of(order[i], 1 - y, c)
        arrived(slot, 1)
        arrived(slot, 2)
        aside(order[i], 1 - y).start()

    for i in range(1, DEPTH):
        relay(i, 1)
        over(order[i], 1).start()
        work(order[i - 1], y)
        relay(i, 2)
        over(order[i], 2).start()
        finish_across(i - 1)
        relay(i, 0)
        aside(order[i], y).start()
        relay(i, 3)
        work(order[i - 1], 1 - y)
    work(order[DEPTH - 1], y)
    finish_across(DEPTH - 1)
    work(order[DEPTH - 1], 1 - y)

    query = (acc[...] * head_scale).astype(jnp.bfloat16)
    query = jnp.dot(select, query, preferred_element_type=jnp.float32)
    q_send[...] = query.astype(jnp.bfloat16).reshape(q_send.shape)
    spread(lambda peer: q_send.at[peer], q_got, q_sem)
    q_got[me] = q_send[me]
    for k in range(1, members // 2):
        to_owner(k, (me + 2 * k) % members // 2).wait()
    fresh_kv = jnp.sum(kv_got[...].astype(jnp.float32), axis=0).astype(jnp.bfloat16)
    fresh_kv = fresh_kv.astype(jnp.float32)
    cache_copy.wait()
    for zz in range(DEPTH):
        for piece in range(3):
            over_sent = (piece > 0) | (zz == z)

            @pl.when(over_sent)
            def _():
                over(zz, piece).wait_send()

        aside(zz, 0).wait_send()
        aside(zz, 1).wait_send()

        @pl.when((z < DEPTH - 1) & (zz <= z))
        def _():
            for piece in range(4):
                up(zz, piece).wait_send()

        @pl.when((z > 0) & (zz >= z))
        def _():
            for piece in range(4):
                down(zz, piece).wait_send()

    collect(lambda peer: q_send.at[peer], q_got, q_sem)
    shape = (members * PAD, members * PAD)
    to = lax.broadcasted_iota(jnp.int32, shape, 0)
    of = lax.broadcasted_iota(jnp.int32, shape, 1)
    turn = ((to & (PAD - 1)) * PAD + (to >> 4)) == of
    turn = jnp.where(turn, 1.0, 0.0).astype(jnp.bfloat16)
    flat = q_got[...].reshape(members * PAD, q_got.shape[2])
    by_row = jnp.dot(turn, flat, preferred_element_type=jnp.float32)
    local = rows // members
    head = cache.shape[2] // 2
    att_rows[...] = jnp.zeros_like(att_rows)
    for r in range(local):
        span = slice(r * PAD, (r + 1) * PAD)
        q32 = jnp.concatenate([by_row[span, 0:head], by_row[span, head : 2 * head]], axis=0)
        scores = lax.dot_general(
            q32.astype(jnp.bfloat16),
            cache[r, :, 0:head],
            (((1,), (1,)), ((), ())),
            preferred_element_type=jnp.float32,
        )
        fresh = jnp.sum(q32 * fresh_kv[r : r + 1, 0:head], axis=1, keepdims=True)
        slots = lax.broadcasted_iota(jnp.int32, scores.shape, 1)
        valid = slots < lengths[r]
        scores = jnp.where(valid, scores, -1e30)
        peak = jnp.maximum(jnp.max(scores, axis=1, keepdims=True), fresh)
        weights = jnp.where(valid, jnp.exp(scores - peak), 0.0)
        fresh_w = jnp.exp(fresh - peak)
        total = jnp.sum(weights, axis=1, keepdims=True) + fresh_w
        probs = (weights / total).astype(jnp.bfloat16)
        fresh_p = (fresh_w / total).astype(jnp.bfloat16).astype(jnp.float32)
        mixed = jnp.dot(probs, cache[r, :, head : 2 * head], preferred_element_type=jnp.float32)
        mixed = (mixed + fresh_p * fresh_kv[r : r + 1, head : 2 * head]).astype(jnp.bfloat16)
        att_rows[span, 0:head] = mixed[0:PAD]
        att_rows[span, head : 2 * head] = mixed[PAD : 2 * PAD]
    back = jnp.dot(turn, att_rows[...], preferred_element_type=jnp.float32)
    att_out[...] = back.astype(jnp.bfloat16).reshape(att_out.shape)


def query_call(x, note, wq, kvw, cache, lengths, members, head_scale):
    rows, width = x.shape
    cols = wq.shape[1]
    vmem = pl.BlockSpec(memory_space=pltpu.VMEM)
    hbm = pl.BlockSpec(memory_space=pl.ANY)
    swap = (members, PAD, cols)
    kv_cols = kvw.shape[1]
    dma = pltpu.SemaphoreType.DMA
    return pl.pallas_call(
        lambda *refs: query_kernel(head_scale, *refs),
        out_shape=jax.ShapeDtypeStruct(swap, jnp.bfloat16),
        in_specs=[hbm, vmem, hbm, hbm, hbm, pl.BlockSpec(memory_space=pltpu.SMEM)],
        out_specs=vmem,
        scratch_shapes=[
            pltpu.VMEM((members, rows, width), jnp.bfloat16),
            pltpu.VMEM((members,) + note.shape, jnp.float32),
            pltpu.VMEM((members, width, cols), jnp.bfloat16),
            pltpu.VMEM(kvw.shape, jnp.bfloat16),
            pltpu.VMEM(cache.shape, jnp.bfloat16),
            pltpu.VMEM((members * PAD, cols), jnp.bfloat16),
            pltpu.VMEM((rows, cols), jnp.float32),
            pltpu.VMEM((2, rows, 128), jnp.float32),
            pltpu.VMEM(swap, jnp.bfloat16),
            pltpu.VMEM(swap, jnp.bfloat16),
            pltpu.VMEM((members, PAD, kv_cols), jnp.bfloat16),
            pltpu.VMEM((members // 2, PAD, kv_cols), jnp.bfloat16),
            pltpu.VMEM((members // 2, PAD, kv_cols), jnp.bfloat16),
            dma((members,)),
            dma((3,)),
            dma((2, DEPTH, 4)),
            dma((DEPTH, 3)),
            dma((2 * DEPTH,)),
            dma((members, 4)),
            dma((2, members)),
            dma((2, members)),
            dma((2, members)),
            dma((2, members // 2)),
        ],
        compiler_params=pltpu.CompilerParams(
            collective_id=0, has_side_effects=True, vmem_limit_bytes=60 * 1024 * 1024
        ),
    )(x, note, wq, kvw, cache, lengths)


def output_kernel(
    att_ref,
    x_hbm,
    wo_hbm,
    out_ref,
    att_got,
    att,
    wbuf,
    mine,
    c_send,
    c_got,
    y_send,
    y_got,
    z_send,
    z_got,
    x,
    w_sem,
    x_sem,
    att_sem,
    c_sem,
    y_sem,
    z_sem,
):
    members = att_ref.shape[0]
    rows, width = out_ref.shape
    me, z, y, c = place()
    sibling = slot_of(z, y, 1 - c)
    across = slot_of(z, 1 - y, c)
    above = slot_of(jnp.minimum(z + 1, DEPTH - 1), y, c)
    below = slot_of(jnp.maximum(z - 1, 0), y, c)
    order = far_to_near(z)
    parts = pieces(rows)
    lanes = parts + [pl.ds(rows, FIRST)]
    x_copy = pltpu.make_async_copy(x_hbm, x, x_sem)

    def weights_copy(slot):
        start = pl.multiple_of(slot * width, 128)
        return pltpu.make_async_copy(
            wo_hbm.at[:, pl.ds(start, width)], wbuf.at[slot], w_sem.at[slot]
        )

    for zz in order:
        for yy in (1 - y, y):
            for cc in (1 - c, c):
                weights_copy(slot_of(zz, yy, cc)).start()
    x_copy.start()
    meet_all(members, me)

    def swap(k):
        peer = (me + k) % members
        return peer, att_ref.at[peer], att_sem.at[0, peer]

    for k in range(1, members):
        peer, src, sem = swap(k)
        remote(src, att_got.at[me], sem, att_sem.at[1, me], peer).start()
    att_got[me] = att_ref[me]
    for k in range(1, members):
        peer, src, sem = swap(k)
        remote(src, att_got.at[peer], sem, att_sem.at[1, peer], peer).wait()
    gathered = att_got[...].reshape(members * PAD, att.shape[1])
    att[...] = jnp.dot(
        spread_rows(members, rows, rows // members, True),
        gathered, preferred_element_type=jnp.float32
    ).astype(jnp.bfloat16)

    tile = width // 3 if width % 384 == 0 else width

    def product(slot, store):
        weights_copy(slot).wait()

        def one(t, carry):
            cols = pl.ds(pl.multiple_of(t * tile, 128), tile)
            store(
                cols, jnp.dot(att[...], wbuf[slot, :, cols], preferred_element_type=jnp.float32)
            )
            return carry

        lax.fori_loop(0, width // tile, one, 0)

    def aside(p):
        return remote(c_send.at[p], c_got.at[p], c_sem.at[0, p], c_sem.at[1, p], sibling)

    def over(i, k):
        return remote(
            y_send.at[i, parts[k], :],
            y_got.at[i, parts[k], :],
            y_sem.at[0, i, k],
            y_sem.at[1, i, k],
            across,
        )

    def up(zz, k):
        return remote(
            z_send.at[zz, lanes[k], :],
            z_got.at[0, zz, lanes[k], :],
            z_sem.at[0, zz, k],
            z_sem.at[1, zz, k],
            above,
        )

    def down(zz, k):
        return remote(
            z_send.at[zz, lanes[k], :],
            z_got.at[1, zz, lanes[k], :],
            z_sem.at[0, zz, k],
            z_sem.at[2, zz, k],
            below,
        )

    def add(p, k, ref, *place):
        mine[p, parts[k % 3], :] += ref[(*place, lanes[k], slice(None))].astype(jnp.float32)

    def blocks(i):
        for j, yy in enumerate((1 - y, y)):
            p = 2 * i + j

            def to_sibling(cols, value):
                c_send[p, :, cols] = value.astype(jnp.bfloat16)

            product(slot_of(order[i], yy, 1 - c), to_sibling)
            aside(p).start()
        for j, yy in enumerate((1 - y, y)):
            p = 2 * i + j

            def keep(cols, value):
                mine[p, :, cols] = value

            product(slot_of(order[i], yy, c), keep)
            aside(p).wait_recv()
            mine[p] += c_got[p].astype(jnp.float32)
            if j == 0:
                for k in (1, 2):
                    y_send[i, parts[k], :] = mine[p, parts[k], :].astype(jnp.bfloat16)
                    over(i, k).start()

    def pass_on(i, k):
        zz = order[i]
        p = 2 * i + (0 if k == 3 else 1)

        def send(step):
            z_send[zz, lanes[k], :] = mine[p, parts[k % 3], :].astype(jnp.bfloat16)
            step(zz, k).start()

        @pl.when(zz > z)
        def _():
            @pl.when(z > 0)
            def _():
                up(zz, k).wait_recv()
                add(p, k, z_got, 0, zz)

            send(up)

        @pl.when(zz < z)
        def _():
            @pl.when(z < DEPTH - 1)
            def _():
                down(zz, k).wait_recv()
                add(p, k, z_got, 1, zz)

            send(down)

    def close(k):
        p = 2 * DEPTH - 2 + (0 if k == 3 else 1)

        @pl.when(z > 0)
        def _():
            up(z, k).wait_recv()
            add(p, k, z_got, 0, z)

        @pl.when(z < DEPTH - 1)
        def _():
            down(z, k).wait_recv()
            add(p, k, z_got, 1, z)

    def heads(i):
        pass_on(i, 3)
        pass_on(i, 0)

    def tails(i):
        for k in (1, 2):
            over(i, k).wait_recv()
            add(2 * i + 1, k, y_got, i)
            pass_on(i, k)

    blocks(0)
    blocks(1)
    heads(0)
    blocks(2)
    heads(1)
    tails(0)
    blocks(3)
    heads(2)
    tails(1)
    tails(2)
    last = DEPTH - 1
    close(3)
    y_send[last, parts[0], :] = mine[2 * last, parts[0], :].astype(jnp.bfloat16)
    over(last, 0).start()
    close(0)
    x_copy.wait()
    for k in (1, 2, 0):
        over(last, k).wait_recv()
        add(2 * last + 1, k, y_got, last)
        if k > 0:
            close(k)
        total = x[parts[k], :].astype(jnp.float32) + mine[2 * last + 1, parts[k], :]
        out_ref[parts[k], :] = total.astype(jnp.bfloat16)
    for i in range(DEPTH):
        over(i, 1).wait_send()
        over(i, 2).wait_send()
        aside(2 * i).wait_send()
        aside(2 * i + 1).wait_send()
    over(last, 0).wait_send()
    for i in range(last):
        for k in range(4):
            up(order[i], k).wait_send()


def output_call(att, x, wo, members):
    rows, width = x.shape
    depth = wo.shape[0]
    vmem = pl.BlockSpec(memory_space=pltpu.VMEM)
    dma = pltpu.SemaphoreType.DMA
    hbm = pl.BlockSpec(memory_space=pl.ANY)
    block = (rows, width)
    tall = (rows + FIRST, width)
    return pl.pallas_call(
        output_kernel,
        out_shape=jax.ShapeDtypeStruct(block, jnp.bfloat16),
        in_specs=[vmem, hbm, hbm],
        out_specs=vmem,
        scratch_shapes=[
            pltpu.VMEM(att.shape, jnp.bfloat16),
            pltpu.VMEM((rows, depth), jnp.bfloat16),
            pltpu.VMEM((members, depth, width), jnp.bfloat16),
            pltpu.VMEM((2 * DEPTH,) + block, jnp.float32),
            pltpu.VMEM((2 * DEPTH,) + block, jnp.bfloat16),
            pltpu.VMEM((2 * DEPTH,) + block, jnp.bfloat16),
            pltpu.VMEM((DEPTH,) + block, jnp.bfloat16),
            pltpu.VMEM((DEPTH,) + block, jnp.bfloat16),
            pltpu.VMEM((DEPTH,) + tall, jnp.bfloat16),
            pltpu.VMEM((2, DEPTH) + tall, jnp.bfloat16),
            pltpu.VMEM(block, jnp.bfloat16),
            dma((members,)),
            dma,
            dma((2, members)),
            dma((2, 2 * DEPTH)),
            dma((2, DEPTH, 3)),
            dma((3, DEPTH, 4)),
        ],
        compiler_params=pltpu.CompilerParams(
            collective_id=1, has_side_effects=True, vmem_limit_bytes=60 * 1024 * 1024
        ),
    )(att, x, wo)


def fast_device(
    hidden_state, norm_gain, query_weight, keyval_weight, out_weight, cache_entries, cache_lengths
):
    members = lax.axis_size("gx")
    rows_all, width = hidden_state.shape
    head_size = keyval_weight.shape[1] // 2
    state32 = hidden_state.astype(jnp.float32)
    sums = jnp.stack([jnp.sum(state32, axis=1), jnp.sum(state32 * state32, axis=1)])
    sums = jnp.pad(sums, ((0, 0), (0, 256 - rows_all))).reshape(4, 128)
    note = jnp.concatenate([sums, norm_gain.reshape(-1, 128)], axis=0)
    note = jnp.pad(note, ((0, -note.shape[0] % 8), (0, 0)))
    att = query_call(
        hidden_state,
        note,
        query_weight,
        keyval_weight,
        cache_entries,
        cache_lengths,
        members,
        head_size ** (-0.5),
    )
    return output_call(att, hidden_state, out_weight, members)


def on_device(hidden_state, *others):
    members = lax.axis_size("gx")
    rows_all, width = hidden_state.shape
    fits = width % 128 == 0 and 128 < rows_all <= 256 and rows_all % 32 == 0
    paired = others[1].shape[1] == others[2].shape[1] and members == PAD
    if members == 4 * DEPTH and fits and paired and rows_all // members <= PAD:
        return fast_device(hidden_state, *others)
    return plain_device(hidden_state, *others)


def solution(mesh):
    in_specs = (
        P("groups", "gx"),
        P("gx"),
        P(None, "gx"),
        P("gx", None),
        P("gx", None),
        P(("groups", "gx"), None, None),
        P(("groups", "gx")),
    )
    out_specs = P("groups", "gx")
    return jax.shard_map(
        on_device, mesh=mesh, in_specs=in_specs, out_specs=out_specs, check_vma=False
    )
```
